256 devices in a mesh: rows: 64 (over z, y, core), cols: 4 (over x).
Axes of the slice: x: 4, y: 4, z: 8, core: 2. Of those that a mesh axis runs over, the one named last changes fastest.
Arguments:
- points: float32 [65536, 1024], P('rows', 'cols'), may hold values from -6 to 6
- pivots: int32 [2, 512], replicated, may hold values from 0 to 65535, as said below
- targets: float32 [65536, 256], P('rows', 'cols'), may hold values from -6 to 6
Outputs:
- factor: float32 [65536, 1024], P(('rows', 'cols'))
- projection: float32 [1024, 256], P(None, 'cols')
The draws below stay inside these ranges and needn't reach their ends.
Inputs may be any that keep to these rules, and one draw needn't show every extreme that they name: All 1024 indices of both blocks are distinct. The points of one index of rows (an aligned run of 1024 indices) hold at most 64 pivots of the two blocks together, and in every draw some index of rows holds exactly 64.
All inputs are finite; a program needn't handle non-finite values.
Results may differ from the reference program's by a relative error of at most 0.0003.
Values sent between devices are 32-bit elements; how exact they have to be, the bound alone decides.
A program may use at most 64 MiB of HBM per device.

```python
import math
import jax
import jax.numpy as jnp
from jax import lax

E = 1024
BLOCK = 512
TGT = 256
ROWS_PER_SHARD = 1024
NPTS = 65536
MOST = 64


def draw_pivots(key, part):
    holding_device_numbers = NPTS // ROWS_PER_SHARD
    most = MOST
    keys = jax.random.split(jax.random.fold_in(key, 17), 5)
    threshold_amount = jax.random.randint(keys[0], (holding_device_numbers,), 0, 4)
    preferred_points = jax.random.randint(keys[1], (), 0, holding_device_numbers)
    random_jitter = jax.random.randint(keys[2], (holding_device_numbers, most), 0, 1024)
    extra_multiplier = jnp.where(jnp.arange(holding_device_numbers) == preferred_points, 4096, 0)
    selection_criterion = random_jitter + threshold_amount[:, None] * 256 + extra_multiplier[:, None]
    distinct = selection_criterion * (holding_device_numbers * most) + jnp.arange(holding_device_numbers * most).reshape(holding_device_numbers, most)
    _, chosen = lax.top_k(distinct.reshape(-1), 2 * BLOCK)
    slot_owner = chosen // most
    slot = chosen % most
    shuffled = jax.random.randint(keys[3], (holding_device_numbers, ROWS_PER_SHARD), 0, 2 ** 18) * ROWS_PER_SHARD + jnp.arange(ROWS_PER_SHARD)[None, :]
    order = jnp.argsort(shuffled, axis=1, stable=True).astype(jnp.int32)
    inside = order[slot_owner, slot]
    position_list = slot_owner * ROWS_PER_SHARD + inside
    mixing = jax.random.permutation(keys[4], 2 * BLOCK)
    return position_list[mixing].reshape(2, BLOCK).astype(jnp.int32)


def shard_levels(rng, shape, shards, low, top_value):
    factor_of = 1.0
    for dim, parts in shards:
        draws = jax.random.uniform(jax.random.fold_in(jax.random.fold_in(rng, 6), dim), (parts,), jnp.float32, low / len(shards), top_value / len(shards))
        factor_of = factor_of * jnp.repeat(jnp.exp(draws), shape[dim] // parts).reshape((-1,) + (1,) * (len(shape) - 1 - dim))
    return factor_of


def bell_draw(rng, extent, scale, bound, shards=(), kind=jnp.bfloat16):
    values = jax.random.normal(rng, extent, jnp.float32) * scale
    if len(shards) > 0:
        values = shard_levels(rng, extent, shards, -0.22, 0.18) * values
    return jnp.clip(values, min=-bound, max=bound).astype(kind)


def setup_inputs(seed: int = 0) -> dict:
    key_list = jax.random.split(jax.random.key(seed), 4)
    points = bell_draw(key_list[0], (NPTS, E), 1.0, 6.0, ((0, 64), (1, 4)), jnp.float32)
    pivots = draw_pivots(jax.random.fold_in(key_list[3], 71), 0)
    targets = bell_draw(key_list[2], (NPTS, TGT), 1.0, 6.0, ((0, 64), (1, 4)), jnp.float32)
    return dict(points=points, pivots=pivots, targets=targets)


RIDGE = 0.001

def right_side_solve(low, values):
    return lax.linalg.triangular_solve(low, values, left_side=False, lower=True, transpose_a=True)

def reference(points, pivots, targets):
    highest = lax.Precision.HIGHEST
    block = pivots.shape[1]
    flat = pivots.reshape(-1)
    chosen = points[flat]
    norms = lax.optimization_barrier(jnp.sum(points * points, axis=1))
    chosen_norms = lax.optimization_barrier(jnp.sum(chosen * chosen, axis=1))
    cross = jnp.dot(points.astype(jnp.float32), chosen.T.astype(jnp.float32), precision=highest, preferred_element_type=jnp.float32)
    dist = norms[:, None] + chosen_norms[None, :] - 2.0 * cross
    kern = jnp.exp(-dist / (2.0 * E))
    first = kern[:, :block]
    second = kern[:, block:]
    identity = jnp.eye(block, dtype=jnp.float32)
    low_one = jnp.linalg.cholesky(first[pivots[0]] + RIDGE * identity)
    factor_one = right_side_solve(low_one, first)
    crossed = factor_one[pivots[1]]
    resid = second - jnp.dot(factor_one.astype(jnp.float32), crossed.T.astype(jnp.float32), precision=highest, preferred_element_type=jnp.float32)
    low_two = jnp.linalg.cholesky(resid[pivots[1]] + RIDGE * identity)
    second_lower_matrix = right_side_solve(low_two, resid)
    factor = jnp.concatenate([factor_one, second_lower_matrix], axis=1)
    projection = jnp.dot(factor.T.astype(jnp.float32), targets.astype(jnp.float32), precision=highest, preferred_element_type=jnp.float32) / math.sqrt(NPTS)
    return (factor, projection)
```

```python
import functools

import jax
import jax.numpy as jnp
from jax import lax
from jax.experimental import pallas as pl
from jax.experimental.pallas import tpu as pltpu
from jax.sharding import PartitionSpec as P

F32, BF16 = jnp.float32, jnp.bfloat16
MESH = pl.DeviceIdType.MESH
VMEM = pltpu.VMEM
HI = lax.Precision.HIGHEST
NT = (((1,), (1,)), ((), ()))
SUB, BLK, NB = 8, 128, 8
Q = NB * BLK
OWN = 256
RIDGE = 0.001

def lanes(x, c):
    return jnp.broadcast_to(x[:, c:c + 1], (SUB, BLK))

def sublanes(x, s):
    return jnp.broadcast_to(x[s:s + 1, :], (SUB, BLK))

def small_factor(e):
    low, inv = {}, [None] * SUB
    for k in range(0, SUB, 2):
        a, b, c = e[k, k], e[k + 1, k], e[k + 1, k + 1]
        ra, rd = lax.rsqrt(a), lax.rsqrt(a * c - b * b)
        inv[k], inv[k + 1] = ra, a * ra * rd
        low[k + 1, k] = b * ra
        f = ra * rd
        for m in range(k + 2, SUB):
            low[m, k] = e[m, k] * ra
            low[m, k + 1] = (a * e[m, k + 1] - b * e[m, k]) * f
        for n in range(k + 2, SUB):
            for m in range(n, SUB):
                e[m, n] = e[m, n] - low[m, k] * low[n, k] - low[m, k + 1] * low[n, k + 1]
    return low, inv

def chol_inverse(a, emit, side):
    groups = BLK // SUB
    lane = lax.broadcasted_iota(jnp.int32, (SUB, BLK), 1)
    sub = lax.broadcasted_iota(jnp.int32, (SUB, BLK), 0)
    w = [jnp.where(lane == sub + SUB * g, 1.0, 0.0).astype(F32) for g in range(groups)]
    side = list(side)
    for g in range(groups):
        cols = [lanes(a[g], SUB * g + k) for k in range(SUB)]
        low, inv = small_factor({(m, k): sublanes(cols[k], m) for k in range(SUB) for m in range(k, SUB)})
        us, ws = [], []
        for k in range(SUB):
            u, x = sublanes(a[g], k), sublanes(w[g], k)
            for j in range(k):
                u, x = u - us[j] * low[k, j], x - ws[j] * low[k, j]
            us.append(u * inv[k])
            ws.append(x * inv[k])
            emit(SUB * g + k, ws[k])
        for i in range(g + 1, groups):
            vs = []
            for k in range(SUB):
                v = lanes(a[i], SUB * g + k)
                for j in range(k):
                    v = v - vs[j] * low[k, j]
                vs.append(v * inv[k])
            ai, wi = a[i], w[i]
            for k in range(SUB):
                ai, wi = ai - vs[k] * us[k], wi - vs[k] * ws[k]
            a[i], w[i] = ai, wi
        take = -(-len(side) // (groups - g))
        for job in side[:take]:
            job()
        side = side[take:]

def dot_nt(a, b, precision=HI):
    return lax.dot_general(a, b, NT, precision=precision, preferred_element_type=F32)

def split(x):
    hi = x.astype(BF16)
    return hi, (x - hi.astype(F32)).astype(BF16)

def dot3(ah, al, bh, bl):
    d = functools.partial(lax.dot_general, dimension_numbers=NT, preferred_element_type=F32)
    return d(ah, bh) + (d(ah, bl) + d(al, bh))

def cuts(lo, hi, step):
    return [(s, min(s + step, hi)) for s in range(lo, hi, step)]

def factor_kernel(piv_ref, kown_ref, fac_ref, low_ref, winv_ref, hi_ref, lo_ref, s_ref, col_ref, row_ref, wt_ref, diag_ref):
    p = piv_ref[...]
    h, l = split(p)
    hi_ref[...] = h
    lo_ref[...] = l
    sq = p * p
    row_ref[...] = dot_nt(jnp.ones((SUB, sq.shape[1]), F32), sq)
    col_ref[...] = jnp.broadcast_to(jnp.sum(sq, axis=1, keepdims=True), (Q, BLK))

    def kern(r0, r1, k):
        c0, c1 = k * BLK, (k + 1) * BLK
        cross = dot3(hi_ref[r0:r1, :], lo_ref[r0:r1, :], hi_ref[c0:c1, :], lo_ref[c0:c1, :])
        dist = col_ref[r0:r1, :] + row_ref[0:1, c0:c1] - 2.0 * cross
        return jnp.exp(dist * (-1.0 / 2048.0))

    def rows_of(r0, r1, c0, c1):
        return low_ref[r0:r1, c0:c1] if r0 < Q else fac_ref[r0 - Q:r1 - Q, c0:c1]

    def put(r0, r1, c0, c1, value):
        if r0 < Q:
            low_ref[r0:r1, c0:c1] = value
        else:
            fac_ref[r0 - Q:r1 - Q, c0:c1] = value

    def schur(r0, r1, k):
        c0, c1 = k * BLK, (k + 1) * BLK
        v = kern(r0, r1, k) if r0 < Q else kown_ref[r0 - Q:r1 - Q, c0:c1]
        if k > 0:
            v = v - dot_nt(rows_of(r0, r1, 0, c0), low_ref[c0:c1, 0:c0])
        s_ref[k % 2, r0:r1, :] = v

    def panel(r0, r1, k):
        put(r0, r1, k * BLK, (k + 1) * BLK, dot_nt(s_ref[k % 2, r0:r1, :], winv_ref[k]))

    eye = jnp.where(lax.broadcasted_iota(jnp.int32, (BLK, BLK), 0) == lax.broadcasted_iota(jnp.int32, (BLK, BLK), 1), RIDGE, 0.0).astype(F32)
    diag_ref[...] = kern(0, BLK, 0) + eye
    for k in range(NB):
        c0, c1 = k * BLK, (k + 1) * BLK
        side = []
        nxt = c1 + BLK
        spans = ([(c1, nxt)] if k + 1 < NB else []) + cuts(nxt, Q, 256) + [(Q, Q + OWN)]
        for r0, r1 in spans:
            if k > 0:
                side.append(functools.partial(panel, r0, r1, k - 1))
            side.append(functools.partial(schur, r0, r1, k))
            if r0 == c1 and r0 < Q:
                def diag_next(r0=r0, r1=r1, k=k):
                    v = kern(r0, r1, k + 1) + eye
                    if k > 0:
                        old = low_ref[r0:r1, 0:k * BLK]
                        v = v - dot_nt(old, old)
                    diag_next_ref[...] = v
                diag_next_ref = s_ref.at[k % 2, c0:c1]
                side.append(diag_next)

        def emit(row, value, k=k):
            winv_ref[k, row:row + 1, :] = value[0:1, :]

        chol_inverse([diag_ref[SUB * g:SUB * (g + 1), :] for g in range(BLK // SUB)], emit, side)
        if k + 1 < NB:
            panel(c1, nxt, k)
            pk = low_ref[c1:nxt, c0:c1]
            diag_ref[...] = s_ref[k % 2, c0:c1, :] - dot_nt(pk, pk)
    panel(Q, Q + OWN, NB - 1)

def factor_call(piv, kown):
    return pl.pallas_call(
        factor_kernel,
        out_shape=(jax.ShapeDtypeStruct((OWN, Q), F32), jax.ShapeDtypeStruct((Q, Q), F32), jax.ShapeDtypeStruct((NB, BLK, BLK), F32)),
        in_specs=[pl.BlockSpec(memory_space=VMEM)] * 2,
        out_specs=[pl.BlockSpec(memory_space=VMEM)] * 3,
        scratch_shapes=[VMEM((Q, 1024), BF16), VMEM((Q, 1024), BF16), VMEM((2, Q + OWN, BLK), F32),
                        VMEM((Q, BLK), F32), VMEM((SUB, Q), F32), VMEM((BLK, BLK), F32), VMEM((BLK, BLK), F32)],
        compiler_params=pltpu.CompilerParams(vmem_limit_bytes=48 << 20),
        name="factor")(piv, kown)

NZ, NY, NX = 8, 4, 4
E, TGT, LOCAL = 1024, 256, 1024
WIDE, TWIDE = E // NX, TGT // NX
HALF, YPART, ZPART = Q // 2, Q // 2 // NY, Q // 2 // NY // NZ
MID = YPART // 2


def picked_rows(ids_ref, points_ref, base, out_ref):
    x = points_ref[...]
    hi = x.astype(BF16)
    rest = x - hi.astype(F32)
    mid = rest.astype(BF16)
    low = (rest - mid.astype(F32)).astype(BF16)
    per_row = ids_ref.shape[1] // BLK
    spot = lax.broadcasted_iota(jnp.int32, (BLK, LOCAL), 1).astype(F32) + base.astype(F32)
    for b in range(NB):
        ids = ids_ref[b // per_row:b // per_row + 1, (b % per_row) * BLK:(b % per_row + 1) * BLK]
        column = jnp.transpose(jnp.broadcast_to(ids.astype(F32), (BLK, BLK)))
        hot = jnp.where(jnp.tile(column, (1, LOCAL // BLK)) == spot, 1.0, 0.0).astype(BF16)
        d = functools.partial(jnp.dot, preferred_element_type=F32)
        out_ref[b * BLK:(b + 1) * BLK, :] = (d(hot, hi) + d(hot, mid)) + d(hot, low)


def gather_kernel(
    ids_ref, points_ref, targets_ref, full_ref, own_ref, tgt_ref,
    pick, from_core, from_y, from_z, own_send, own_recv, tgt_send, tgt_recv,
    core_send, core_recv, y_send, y_recv, z_send, z_recv,
    gz_send, gz_recv, a1_send, a1_recv, b1_send, b1_recv, a2_send, a2_recv, b2_send, b2_recv, fwd_send, fwd_recv,
):
    row, x = lax.axis_index("rows"), lax.axis_index("cols")
    core, y, z = row % 2, (row // 2) % NY, row // (2 * NY)

    def at(z_, y_, core_, x_):
        return ((z_ * NY + y_) * 2 + core_, x_)

    sibling = at(z, y, 1 - core, x)
    xs = [(x + d) % NX for d in range(1, NX)]
    ys = [(y + d) % NY for d in range(1, NY)]
    zs = [(z + d) % NZ for d in range(1, NZ)]
    peers = [sibling] + [at(z, y, core, v) for v in xs] + [at(z, v, core, x) for v in ys] + [at(v, y, core, x) for v in zs]
    barrier = pltpu.get_barrier_semaphore()
    for peer in peers:
        pl.semaphore_signal(barrier, inc=1, device_id=peer, device_id_type=MESH)
    pl.semaphore_wait(barrier, len(peers))

    def send(src, dst, ssem, rsem, peer):
        c = pltpu.make_async_remote_copy(src_ref=src, dst_ref=dst, send_sem=ssem, recv_sem=rsem, device_id=peer, device_id_type=MESH)
        c.start()
        return c

    def part(i, n):
        return pl.ds(pl.multiple_of(i * n, n), n)

    moved = []
    for d, v in enumerate(xs):
        moved.append(send(points_ref.at[part(v, LOCAL // NX), :], own_ref.at[:, part(x, WIDE)], own_send.at[d], own_recv.at[d], at(z, y, core, v)))
        moved.append(send(targets_ref.at[part(v, LOCAL // NX), :], tgt_ref.at[x], tgt_send.at[d], tgt_recv.at[d], at(z, y, core, v)))
    own_ref[:, part(x, WIDE)] = points_ref[part(x, LOCAL // NX), :]
    tgt_ref[x] = targets_ref[part(x, LOCAL // NX), :]

    picked_rows(ids_ref, points_ref, row * LOCAL, pick)

    c = send(pick.at[part(1 - core, HALF), :], from_core, core_send, core_recv, sibling)
    c.wait_recv()
    mine = part(core, HALF)
    pick[mine, :] = pick[mine, :] + from_core[...]
    ysent = []
    for d, v in enumerate(ys):
        ysent.append(send(pick.at[pl.ds(pl.multiple_of(core * HALF + v * YPART, YPART), YPART), :], from_y.at[d], y_send.at[d], y_recv.at[d], at(z, v, core, x)))
    for s in ysent:
        s.wait_recv()
    at_y = pl.multiple_of(core * HALF + y * YPART, YPART)
    pick[pl.ds(at_y, YPART), :] = pick[pl.ds(at_y, YPART), :] + from_y[0] + from_y[1] + from_y[2]
    zsent = []
    for d, v in enumerate(zs):
        zsent.append(send(pick.at[pl.ds(pl.multiple_of(at_y + v * ZPART, ZPART), ZPART), :], from_z.at[d], z_send.at[d], z_recv.at[d], at(v, y, core, x)))
    for s in zsent:
        s.wait_recv()
    at_z = pl.multiple_of(at_y + z * ZPART, ZPART)
    total = pick[pl.ds(at_z, ZPART), :]
    for d in range(NZ - 1):
        total = total + from_z[d]
    cols_me = part(x, WIDE)
    full_ref[pl.ds(at_z, ZPART), cols_me] = total

    gz = [send(full_ref.at[pl.ds(at_z, ZPART), cols_me], full_ref.at[pl.ds(at_z, ZPART), cols_me], gz_send.at[d], gz_recv.at[d], at(v, y, core, x)) for d, v in enumerate(zs)]
    for s in gz:
        s.wait_recv()
    count = 0
    forwards = []

    def forward(rows, cols):
        k = len(forwards)
        forwards.append(send(full_ref.at[rows, cols], full_ref.at[rows, cols], fwd_send.at[k], fwd_recv.at[k], sibling))

    def rows_a(v):
        return pl.ds(pl.multiple_of(core * HALF + v * YPART, MID), MID)

    def rows_b(v):
        return pl.ds(pl.multiple_of(core * HALF + v * YPART + MID, MID), MID)

    everything = pl.ds(0, E)
    a1 = [send(full_ref.at[rows_a(y), cols_me], full_ref.at[rows_a(y), cols_me], a1_send.at[d], a1_recv.at[d], at(z, y, core, v)) for d, v in enumerate(xs)]
    b1 = [send(full_ref.at[rows_b(y), cols_me], full_ref.at[rows_b(y), cols_me], b1_send.at[d], b1_recv.at[d], at(z, v, core, x)) for d, v in enumerate(ys)]
    for s in a1:
        s.wait_recv()
    a2 = [send(full_ref.at[rows_a(y), everything], full_ref.at[rows_a(y), everything], a2_send.at[d], a2_recv.at[d], at(z, v, core, x)) for d, v in enumerate(ys)]
    forward(rows_a(y), everything)
    for s in b1:
        s.wait_recv()
    b2 = []
    for d, v in enumerate(xs):
        for u in range(NY):
            b2.append(send(full_ref.at[rows_b(u), cols_me], full_ref.at[rows_b(u), cols_me], b2_send.at[d, u], b2_recv.at[d, u], at(z, y, core, v)))
    for u in range(NY):
        forward(rows_b(u), cols_me)
    for d in range(NY - 1):
        a2[d].wait_recv()
        forward(rows_a((y + NY - 1 - d) % NY), everything)
    for d in range(NX - 1):
        for u in range(NY):
            b2[d * NY + u].wait_recv()
            forward(rows_b(u), part((x + NX - 1 - d) % NX, WIDE))
    for s in forwards:
        s.wait_recv()
    for s in moved:
        s.wait_recv()
    for s in moved + [c] + ysent + zsent + gz + a1 + b1 + a2 + b2 + forwards:
        s.wait_send()


def gather_call(pivots, points, targets):
    dma = pltpu.SemaphoreType.DMA
    n_fwd = 1 + NY + (NY - 1) + (NX - 1) * NY
    return pl.pallas_call(
        gather_kernel,
        out_shape=(
            jax.ShapeDtypeStruct((Q, E), F32),
            jax.ShapeDtypeStruct((OWN, E), F32),
            jax.ShapeDtypeStruct((NX, OWN, TWIDE), F32),
        ),
        in_specs=[pl.BlockSpec(memory_space=VMEM)] * 3,
        out_specs=[pl.BlockSpec(memory_space=VMEM)] * 3,
        scratch_shapes=[
            VMEM((Q, WIDE), F32), VMEM((HALF, WIDE), F32), VMEM((NY - 1, YPART, WIDE), F32), VMEM((NZ - 1, ZPART, WIDE), F32),
            dma((NX - 1,)), dma((NX - 1,)), dma((NX - 1,)), dma((NX - 1,)),
            dma, dma, dma((NY - 1,)), dma((NY - 1,)), dma((NZ - 1,)), dma((NZ - 1,)),
            dma((NZ - 1,)), dma((NZ - 1,)), dma((NX - 1,)), dma((NX - 1,)), dma((NY - 1,)), dma((NY - 1,)),
            dma((NY - 1,)), dma((NY - 1,)), dma((NX - 1, NY)), dma((NX - 1, NY)), dma((n_fwd,)), dma((n_fwd,)),
        ],
        compiler_params=pltpu.CompilerParams(collective_id=0, has_side_effects=True, vmem_limit_bytes=40 << 20),
        name="pivot_gather",
    )(pivots, points, targets)


def own_kernel(piv_ref, own_ref, tgt_ref, kown_ref, moment_ref):
    p, x = piv_ref[...], own_ref[...]
    row = dot_nt(jnp.ones((SUB, E), F32), p * p)[0:1, :]
    col = jnp.sum(x * x, axis=1, keepdims=True)
    dist = col + row - 2.0 * dot3(*split(x), *split(p))
    kown = jnp.exp(dist * (-0.5 / E))
    kown_ref[...] = kown
    for c in range(NX):
        moment_ref[c * TWIDE:(c + 1) * TWIDE, :] = lax.dot_general(
            tgt_ref[c], kown, (((0,), (0,)), ((), ())), precision=HI, preferred_element_type=F32)


def own_call(piv, own, tgt):
    return pl.pallas_call(
        own_kernel,
        out_shape=(jax.ShapeDtypeStruct((OWN, Q), F32), jax.ShapeDtypeStruct((TGT, Q), F32)),
        in_specs=[pl.BlockSpec(memory_space=VMEM)] * 3,
        out_specs=[pl.BlockSpec(memory_space=VMEM)] * 2,
        compiler_params=pltpu.CompilerParams(vmem_limit_bytes=48 << 20),
        name="own_kernel_rows",
    )(piv, own, tgt)


def project_kernel(moment_ref, low_ref, winv_ref, out_ref, x_ref):
    x_ref[...] = moment_ref[...]
    for k in range(NB):
        c0, c1 = k * BLK, (k + 1) * BLK
        s = dot_nt(x_ref[:, c0:c1], winv_ref[k])
        out_ref[c0:c1, :] = jnp.transpose(s * (1.0 / 256.0))
        for c in range(c1, Q, BLK):
            x_ref[:, c:c + BLK] = x_ref[:, c:c + BLK] - dot_nt(s, low_ref[c:c + BLK, c0:c1])


def project_call(moment, low, winv):
    return pl.pallas_call(
        project_kernel,
        out_shape=jax.ShapeDtypeStruct((Q, TWIDE), F32),
        in_specs=[pl.BlockSpec(memory_space=VMEM)] * 3,
        out_specs=pl.BlockSpec(memory_space=VMEM),
        scratch_shapes=[VMEM((TWIDE, Q), F32)],
        compiler_params=pltpu.CompilerParams(vmem_limit_bytes=32 << 20),
        name="projection_solve",
    )(moment, low, winv)


def shards(points, pivots, targets):
    piv, own, tgt = gather_call(pivots, points, targets)
    kown, moment = own_call(piv, own, tgt)
    part = lax.psum_scatter(moment, "cols", scatter_dimension=0, tiled=True)
    moment = lax.psum(part, "rows")
    factor, low, winv = factor_call(piv, kown)
    return factor, project_call(moment, low, winv)


def solution(mesh):
    return jax.shard_map(
        shards,
        mesh=mesh,
        in_specs=(P("rows", "cols"), P(), P("rows", "cols")),
        out_specs=(P(("rows", "cols"), None), P(None, "cols")),
        check_vma=False,
    )
```

```python
import functools

import jax
import jax.numpy as jnp
from jax import lax
from jax.experimental import pallas as pl
from jax.experimental.pallas import tpu as pltpu
from jax.sharding import PartitionSpec as P

F32, BF16 = jnp.float32, jnp.bfloat16
MESH = pl.DeviceIdType.MESH
VMEM = pltpu.VMEM

HI = lax.Precision.HIGHEST
NT = (((1,), (1,)), ((), ()))
SUB, BLK, NB = 8, 128, 8
Q = NB * BLK
OWN = 256
RIDGE = 0.001
NZ, NY, NX = 8, 4, 4
E, TGT, LOCAL = 1024, 256, 1024
WIDE, TWIDE = E // NX, TGT // NX


def lanes(x, c):
    return jnp.broadcast_to(x[:, c:c + 1], (SUB, BLK))


def sublanes(x, s):
    return jnp.broadcast_to(x[s:s + 1, :], (SUB, BLK))


def small_factor(e):
    low, inv = {}, [None] * SUB
    for k in range(0, SUB, 2):
        a, b, c = e[k, k], e[k + 1, k], e[k + 1, k + 1]
        ra, rd = lax.rsqrt(a), lax.rsqrt(a * c - b * b)
        inv[k], inv[k + 1] = ra, a * ra * rd
        low[k + 1, k] = b * ra
        f = ra * rd
        for m in range(k + 2, SUB):
            low[m, k] = e[m, k] * ra
            low[m, k + 1] = (a * e[m, k + 1] - b * e[m, k]) * f
        for n in range(k + 2, SUB):
            for m in range(n, SUB):
                e[m, n] = e[m, n] - low[m, k] * low[n, k] - low[m, k + 1] * low[n, k + 1]
    return low, inv


def chol_inverse(a, emit, side):
    groups = BLK // SUB
    lane = lax.broadcasted_iota(jnp.int32, (SUB, BLK), 1)
    sub = lax.broadcasted_iota(jnp.int32, (SUB, BLK), 0)
    w = [jnp.where(lane == sub + SUB * g, 1.0, 0.0).astype(F32) for g in range(groups)]
    side = list(side)
    for g in range(groups):
        cols = [lanes(a[g], SUB * g + k) for k in range(SUB)]
        low, inv = small_factor({(m, k): sublanes(cols[k], m) for k in range(SUB) for m in range(k, SUB)})
        us, ws = [], []
        for k in range(SUB):
            u, x = sublanes(a[g], k), sublanes(w[g], k)
            for j in range(k):
                u, x = u - us[j] * low[k, j], x - ws[j] * low[k, j]
            us.append(u * inv[k])
            ws.append(x * inv[k])
            emit(SUB * g + k, ws[k])
        for i in range(g + 1, groups):
            vs = []
            for k in range(SUB):
                v = lanes(a[i], SUB * g + k)
                for j in range(k):
                    v = v - vs[j] * low[k, j]
                vs.append(v * inv[k])
            ai, wi = a[i], w[i]
            for k in range(SUB):
                ai, wi = ai - vs[k] * us[k], wi - vs[k] * ws[k]
            a[i], w[i] = ai, wi
        take = -(-len(side) // (groups - g))
        for job in side[:take]:
            job()
        side = side[take:]


def dot_nt(a, b, precision=HI):
    return lax.dot_general(a, b, NT, precision=precision, preferred_element_type=F32)


def split(x):
    hi = x.astype(BF16)
    return hi, (x - hi.astype(F32)).astype(BF16)


def dot3(ah, al, bh, bl):
    d = functools.partial(lax.dot_general, dimension_numbers=NT, preferred_element_type=F32)
    return d(ah, bh) + (d(ah, bl) + d(al, bh))


def cuts(lo, hi, step):
    return [(s, min(s + step, hi)) for s in range(lo, hi, step)]


def factor_kernel(
    piv_hbm, own_hbm, tgt_hbm, fac_ref, moment_ref,
    x_ref, t_ref, tt_ref, hi_ref, lo_ref, low_ref, winv_ref, s_ref, col_ref, row_ref, diag_ref, sems,
):
    loads = [pltpu.make_async_copy(piv_hbm.at[b * BLK:(b + 1) * BLK, :], x_ref.at[b * BLK:(b + 1) * BLK, :], sems.at[b]) for b in range(NB)]
    loads.append(pltpu.make_async_copy(own_hbm, x_ref.at[Q:Q + OWN, :], sems.at[NB]))
    loads.append(pltpu.make_async_copy(tgt_hbm, t_ref, sems.at[NB + 1]))
    for c in loads:
        c.start()

    def prepare(b):
        loads[b].wait()
        for r0, r1 in cuts(b * BLK, (b + 1) * BLK if b < NB else Q + OWN, BLK):
            v = x_ref[r0:r1, :]
            hi_ref[r0:r1, :], lo_ref[r0:r1, :] = split(v)
            norms = jnp.broadcast_to(jnp.sum(v * v, axis=1, keepdims=True), (BLK, BLK))
            col_ref[r0:r1, :] = norms
            if b < NB:
                row_ref[:, r0:r1] = jnp.transpose(norms)[0:SUB, :]

    def turn_targets():
        loads[NB + 1].wait()
        for c in range(NX):
            tt_ref[c * TWIDE:(c + 1) * TWIDE, :] = jnp.transpose(t_ref[c])

    def kern(r0, r1, k):
        c0, c1 = k * BLK, (k + 1) * BLK
        cross = dot3(hi_ref[r0:r1, :], lo_ref[r0:r1, :], hi_ref[c0:c1, :], lo_ref[c0:c1, :])
        return jnp.exp((col_ref[r0:r1, :] + row_ref[0:1, c0:c1] - 2.0 * cross) * (-0.5 / E))

    def done(r0, r1, c0, c1):
        return (low_ref, r0, r1) if r0 < Q else (fac_ref, r0 - Q, r1 - Q)

    def schur(r0, r1, k):
        c0, c1 = k * BLK, (k + 1) * BLK
        v = kern(r0, r1, k)
        if k > 0:
            ref, a, b = done(r0, r1, 0, c0)
            v = v - dot_nt(ref[a:b, 0:c0], low_ref[c0:c1, 0:c0])
        s_ref[k % 2, r0:r1, :] = v

    def panel(r0, r1, k):
        c0, c1 = k * BLK, (k + 1) * BLK
        ref, a, b = done(r0, r1, c0, c1)
        ref[a:b, c0:c1] = dot_nt(s_ref[k % 2, r0:r1, :], winv_ref[k])

    def moment(k):
        c0, c1 = k * BLK, (k + 1) * BLK
        moment_ref[:, c0:c1] = jnp.dot(tt_ref[...], fac_ref[:, c0:c1], precision=HI, preferred_element_type=F32)

    rows, columns = (lax.broadcasted_iota(jnp.int32, (BLK, BLK), d) for d in (0, 1))
    ridge = jnp.where(rows == columns, RIDGE, 0.0).astype(F32)

    def next_diagonal(k):
        r0, r1 = (k + 1) * BLK, (k + 2) * BLK
        v = kern(r0, r1, k + 1) + ridge
        if k > 0:
            old = low_ref[r0:r1, 0:k * BLK]
            v = v - dot_nt(old, old)
        s_ref[k % 2, k * BLK:(k + 1) * BLK, :] = v

    do = functools.partial
    prepare(0)
    diag_ref[...] = kern(0, BLK, 0) + ridge
    for k in range(NB):
        c0, c1, c2 = k * BLK, (k + 1) * BLK, (k + 2) * BLK
        side = []
        if k == 0:
            side += [do(prepare, b) for b in range(1, NB + 1)] + [turn_targets]
        spans = ([(c1, c2)] if k + 1 < NB else []) + cuts(c2, Q, 256) + [(Q, Q + OWN)]
        for r0, r1 in spans:
            if k > 0:
                side.append(do(panel, r0, r1, k - 1))
            side.append(do(schur, r0, r1, k))
            if r0 == c1 and r0 < Q:
                side.append(do(next_diagonal, k))
        if k > 0:
            side.append(do(moment, k - 1))

        def emit(row, value, k=k):
            winv_ref[k, row:row + 1, :] = value[0:1, :]

        chol_inverse([diag_ref[SUB * g:SUB * (g + 1), :] for g in range(BLK // SUB)], emit, side)
        if k + 1 < NB:
            panel(c1, c2, k)
            last = low_ref[c1:c2, c0:c1]
            diag_ref[...] = s_ref[k % 2, c0:c1, :] - dot_nt(last, last)
    panel(Q, Q + OWN, NB - 1)
    moment(NB - 1)


def factor_call(piv, own, tgt):
    rows = Q + OWN
    return pl.pallas_call(
        factor_kernel,
        out_shape=(jax.ShapeDtypeStruct((OWN, Q), F32), jax.ShapeDtypeStruct((TGT, Q), F32)),
        in_specs=[pl.BlockSpec(memory_space=pl.ANY)] * 3,
        out_specs=[pl.BlockSpec(memory_space=VMEM)] * 2,
        scratch_shapes=[
            VMEM((rows, E), F32), VMEM((NX, OWN, TWIDE), F32), VMEM((TGT, OWN), F32), VMEM((rows, E), BF16), VMEM((rows, E), BF16),
            VMEM((Q, Q), F32), VMEM((NB, BLK, BLK), F32), VMEM((2, rows, BLK), F32), VMEM((rows, BLK), F32), VMEM((SUB, Q), F32),
            VMEM((BLK, BLK), F32), pltpu.SemaphoreType.DMA((NB + 2,)),
        ],
        compiler_params=pltpu.CompilerParams(vmem_limit_bytes=48 << 20),
        name="factor",
    )(piv, own, tgt)


HALF, YPART, ZPART = Q // 2, Q // 2 // NY, Q // 2 // NY // NZ
MID = YPART // 2


def picked_rows(ids_ref, points_ref, base, out_ref):
    x = points_ref[...]
    hi = x.astype(BF16)
    rest = x - hi.astype(F32)
    mid = rest.astype(BF16)
    low = (rest - mid.astype(F32)).astype(BF16)
    per_row = ids_ref.shape[1] // BLK
    spot = lax.broadcasted_iota(jnp.int32, (BLK, LOCAL), 1).astype(F32) + base.astype(F32)
    for b in range(NB):
        ids = ids_ref[b // per_row:b // per_row + 1, (b % per_row) * BLK:(b % per_row + 1) * BLK]
        column = jnp.transpose(jnp.broadcast_to(ids.astype(F32), (BLK, BLK)))
        hot = jnp.where(jnp.tile(column, (1, LOCAL // BLK)) == spot, 1.0, 0.0).astype(BF16)
        d = functools.partial(jnp.dot, preferred_element_type=F32)
        out_ref[b * BLK:(b + 1) * BLK, :] = (d(hot, hi) + d(hot, mid)) + d(hot, low)


def gather_kernel(
    ids_ref, points_ref, targets_ref, full_ref, own_ref, tgt_ref,
    pick, from_core, from_y, from_z, own_send, own_recv, tgt_send, tgt_recv,
    core_send, core_recv, y_send, y_recv, z_send, z_recv,
    gz_send, gz_recv, a1_send, a1_recv, b1_send, b1_recv, a2_send, a2_recv, b2_send, b2_recv, fwd_send, fwd_recv,
):
    row, x = lax.axis_index("rows"), lax.axis_index("cols")
    core, y, z = row % 2, (row // 2) % NY, row // (2 * NY)

    def at(z_, y_, core_, x_):
        return ((z_ * NY + y_) * 2 + core_, x_)

    sibling = at(z, y, 1 - core, x)
    xs = [(x + d) % NX for d in range(1, NX)]
    ys = [(y + d) % NY for d in range(1, NY)]
    zs = [(z + d) % NZ for d in range(1, NZ)]
    peers = [sibling] + [at(z, y, core, v) for v in xs] + [at(z, v, core, x) for v in ys] + [at(v, y, core, x) for v in zs]
    barrier = pltpu.get_barrier_semaphore()
    for peer in peers:
        pl.semaphore_signal(barrier, inc=1, device_id=peer, device_id_type=MESH)
    pl.semaphore_wait(barrier, len(peers))

    def send(src, dst, ssem, rsem, peer):
        c = pltpu.make_async_remote_copy(src_ref=src, dst_ref=dst, send_sem=ssem, recv_sem=rsem, device_id=peer, device_id_type=MESH)
        c.start()
        return c

    def part(i, n):
        return pl.ds(pl.multiple_of(i * n, n), n)

    moved = []
    for d, v in enumerate(xs):
        moved.append(send(points_ref.at[part(v, LOCAL // NX), :], own_ref.at[:, part(x, WIDE)], own_send.at[d], own_recv.at[d], at(z, y, core, v)))
        moved.append(send(targets_ref.at[part(v, LOCAL // NX), :], tgt_ref.at[x], tgt_send.at[d], tgt_recv.at[d], at(z, y, core, v)))
    own_ref[:, part(x, WIDE)] = points_ref[part(x, LOCAL // NX), :]
    tgt_ref[x] = targets_ref[part(x, LOCAL // NX), :]

    picked_rows(ids_ref, points_ref, row * LOCAL, pick)

    c = send(pick.at[part(1 - core, HALF), :], from_core, core_send, core_recv, sibling)
    c.wait_recv()
    mine = part(core, HALF)
    pick[mine, :] = pick[mine, :] + from_core[...]
    ysent = []
    for d, v in enumerate(ys):
        ysent.append(send(pick.at[pl.ds(pl.multiple_of(core * HALF + v * YPART, YPART), YPART), :], from_y.at[d], y_send.at[d], y_recv.at[d], at(z, v, core, x)))
    for s in ysent:
        s.wait_recv()
    at_y = pl.multiple_of(core * HALF + y * YPART, YPART)
    pick[pl.ds(at_y, YPART), :] = pick[pl.ds(at_y, YPART), :] + from_y[0] + from_y[1] + from_y[2]
    zsent = []
    for d, v in enumerate(zs):
        zsent.append(send(pick.at[pl.ds(pl.multiple_of(at_y + v * ZPART, ZPART), ZPART), :], from_z.at[d], z_send.at[d], z_recv.at[d], at(v, y, core, x)))
    for s in zsent:
        s.wait_recv()
    at_z = pl.multiple_of(at_y + z * ZPART, ZPART)
    total = pick[pl.ds(at_z, ZPART), :]
    for d in range(NZ - 1):
        total = total + from_z[d]
    cols_me = part(x, WIDE)
    full_ref[pl.ds(at_z, ZPART), cols_me] = total

    gz = [send(full_ref.at[pl.ds(at_z, ZPART), cols_me], full_ref.at[pl.ds(at_z, ZPART), cols_me], gz_send.at[d], gz_recv.at[d], at(v, y, core, x)) for d, v in enumerate(zs)]
    for s in gz:
        s.wait_recv()
    count = 0
    forwards = []

    def forward(rows, cols):
        k = len(forwards)
        forwards.append(send(full_ref.at[rows, cols], full_ref.at[rows, cols], fwd_send.at[k], fwd_recv.at[k], sibling))

    def rows_a(v):
        return pl.ds(pl.multiple_of(core * HALF + v * YPART, MID), MID)

    def rows_b(v):
        return pl.ds(pl.multiple_of(core * HALF + v * YPART + MID, MID), MID)

    everything = pl.ds(0, E)
    a1 = [send(full_ref.at[rows_a(y), cols_me], full_ref.at[rows_a(y), cols_me], a1_send.at[d], a1_recv.at[d], at(z, y, core, v)) for d, v in enumerate(xs)]
    b1 = [send(full_ref.at[rows_b(y), cols_me], full_ref.at[rows_b(y), cols_me], b1_send.at[d], b1_recv.at[d], at(z, v, core, x)) for d, v in enumerate(ys)]
    for s in a1:
        s.wait_recv()
    a2 = [send(full_ref.at[rows_a(y), everything], full_ref.at[rows_a(y), everything], a2_send.at[d], a2_recv.at[d], at(z, v, core, x)) for d, v in enumerate(ys)]
    forward(rows_a(y), everything)
    for s in b1:
        s.wait_recv()
    b2 = []
    for d, v in enumerate(xs):
        for u in range(NY):
            b2.append(send(full_ref.at[rows_b(u), cols_me], full_ref.at[rows_b(u), cols_me], b2_send.at[d, u], b2_recv.at[d, u], at(z, y, core, v)))
    for u in range(NY):
        forward(rows_b(u), cols_me)
    for d in range(NY - 1):
        a2[d].wait_recv()
        forward(rows_a((y + NY - 1 - d) % NY), everything)
    for d in range(NX - 1):
        for u in range(NY):
            b2[d * NY + u].wait_recv()
            forward(rows_b(u), part((x + NX - 1 - d) % NX, WIDE))
    for s in forwards:
        s.wait_recv()
    for s in moved:
        s.wait_recv()
    for s in moved + [c] + ysent + zsent + gz + a1 + b1 + a2 + b2 + forwards:
        s.wait_send()


def gather_call(pivots, points, targets):
    dma = pltpu.SemaphoreType.DMA
    n_fwd = 1 + NY + (NY - 1) + (NX - 1) * NY
    return pl.pallas_call(
        gather_kernel,
        out_shape=(
            jax.ShapeDtypeStruct((Q, E), F32),
            jax.ShapeDtypeStruct((OWN, E), F32),
            jax.ShapeDtypeStruct((NX, OWN, TWIDE), F32),
        ),
        in_specs=[pl.BlockSpec(memory_space=VMEM)] * 3,
        out_specs=[pl.BlockSpec(memory_space=VMEM)] * 3,
        scratch_shapes=[
            VMEM((Q, WIDE), F32), VMEM((HALF, WIDE), F32), VMEM((NY - 1, YPART, WIDE), F32), VMEM((NZ - 1, ZPART, WIDE), F32),
            dma((NX - 1,)), dma((NX - 1,)), dma((NX - 1,)), dma((NX - 1,)),
            dma, dma, dma((NY - 1,)), dma((NY - 1,)), dma((NZ - 1,)), dma((NZ - 1,)),
            dma((NZ - 1,)), dma((NZ - 1,)), dma((NX - 1,)), dma((NX - 1,)), dma((NY - 1,)), dma((NY - 1,)),
            dma((NY - 1,)), dma((NY - 1,)), dma((NX - 1, NY)), dma((NX - 1, NY)), dma((n_fwd,)), dma((n_fwd,)),
        ],
        compiler_params=pltpu.CompilerParams(collective_id=0, has_side_effects=True, vmem_limit_bytes=40 << 20),
        name="pivot_gather",
    )(pivots, points, targets)


TP = TWIDE // 2
LHALF = Q // 2


def reduce_kernel(
    in_ref, out_ref, m_ref, core_in, ax_in, by_in, ay_in, bx_in, z_in,
    core_sem, ax_sem, by_sem, ay_sem, bx_sem, z_sem, gz_sem, gy_sem, gc_sem,
):
    row, x = lax.axis_index("rows"), lax.axis_index("cols")
    core, y, z = row % 2, (row // 2) % NY, row // (2 * NY)

    def at(z_, y_, core_, x_):
        return ((z_ * NY + y_) * 2 + core_, x_)

    sibling = at(z, y, 1 - core, x)
    xs = [(x + d) % NX for d in range(1, NX)]
    ys = [(y + d) % NY for d in range(1, NY)]
    zs = [(z + d) % NZ for d in range(1, NZ)]
    to_x = [at(z, y, core, v) for v in xs]
    to_y = [at(z, v, core, x) for v in ys]
    to_z = [at(v, y, core, x) for v in zs]
    barrier = pltpu.get_barrier_semaphore()
    peers = [sibling] + to_x + to_y + to_z
    for peer in peers:
        pl.semaphore_signal(barrier, inc=1, device_id=peer, device_id_type=MESH)
    pl.semaphore_wait(barrier, len(peers))
    started = []

    def send(src, dst, sem, peer):
        c = pltpu.make_async_remote_copy(src_ref=src, dst_ref=dst, send_sem=sem.at[0], recv_sem=sem.at[1], device_id=peer, device_id_type=MESH)
        c.start()
        started.append(c)
        return c

    def arrive(copies):
        for c in copies:
            c.wait_recv()

    def lanes_of(c_, y_):
        return pl.ds(pl.multiple_of(c_ * LHALF + y_ * BLK, BLK), BLK)

    def half(c_):
        return pl.ds(pl.multiple_of(c_ * LHALF, LHALF), LHALF)

    every, first, second = pl.ds(0, NX), pl.ds(0, TP), pl.ds(TP, TP)
    mine, tile = half(core), lanes_of(core, y)
    c = send(in_ref.at[:, :, half(1 - core)], core_in, core_sem, sibling)
    arrive([c])
    m_ref[:, :, mine] = in_ref[:, :, mine] + core_in[...]
    a = [send(m_ref.at[xs[d], first, mine], ax_in.at[d], ax_sem.at[:, d], to_x[d]) for d in range(NX - 1)]
    b = [send(m_ref.at[every, second, lanes_of(core, ys[d])], by_in.at[d], by_sem.at[:, d], to_y[d]) for d in range(NY - 1)]
    arrive(a)
    m_ref[x, first, mine] = m_ref[x, first, mine] + ax_in[0] + ax_in[1] + ax_in[2]
    a = [send(m_ref.at[x, first, lanes_of(core, ys[d])], ay_in.at[d], ay_sem.at[:, d], to_y[d]) for d in range(NY - 1)]
    arrive(b)
    m_ref[every, second, tile] = m_ref[every, second, tile] + by_in[0] + by_in[1] + by_in[2]
    b = [send(m_ref.at[xs[d], second, tile], bx_in.at[d], bx_sem.at[:, d], to_x[d]) for d in range(NX - 1)]
    arrive(a)
    m_ref[x, first, tile] = m_ref[x, first, tile] + ay_in[0] + ay_in[1] + ay_in[2]
    arrive(b)
    m_ref[x, second, tile] = m_ref[x, second, tile] + bx_in[0] + bx_in[1] + bx_in[2]

    def eight(v):
        return pl.ds(pl.multiple_of(v * SUB, SUB), SUB)

    arrive([send(m_ref.at[x, eight(zs[d]), tile], z_in.at[d], z_sem.at[:, d], to_z[d]) for d in range(NZ - 1)])
    total = m_ref[x, eight(z), tile]
    for d in range(NZ - 1):
        total = total + z_in[d]
    out_ref[eight(z), tile] = total * (1.0 / 256.0)
    arrive([send(out_ref.at[eight(z), tile], out_ref.at[eight(z), tile], gz_sem.at[:, d], to_z[d]) for d in range(NZ - 1)])
    a = [send(out_ref.at[:, tile], out_ref.at[:, tile], gy_sem.at[:, d], to_y[d]) for d in range(NY - 1)]
    b = [send(out_ref.at[:, tile], out_ref.at[:, tile], gc_sem.at[:, 0], sibling)]
    for d in range(NY - 1):
        arrive([a[d]])
        block = lanes_of(core, (y + NY - 1 - d) % NY)
        b.append(send(out_ref.at[:, block], out_ref.at[:, block], gc_sem.at[:, d + 1], sibling))
    arrive(b)
    for c in started:
        c.wait_send()


def reduce_call(partial):
    dma = pltpu.SemaphoreType.DMA
    return pl.pallas_call(
        reduce_kernel,
        out_shape=jax.ShapeDtypeStruct((TWIDE, Q), F32),
        in_specs=[pl.BlockSpec(memory_space=VMEM)],
        out_specs=pl.BlockSpec(memory_space=VMEM),
        scratch_shapes=[
            VMEM((NX, TWIDE, Q), F32), VMEM((NX, TWIDE, LHALF), F32), VMEM((NX - 1, TP, LHALF), F32), VMEM((NY - 1, NX, TP, BLK), F32),
            VMEM((NY - 1, TP, BLK), F32), VMEM((NX - 1, TP, BLK), F32), VMEM((NZ - 1, SUB, BLK), F32),
            dma((2,)), dma((2, NX - 1)), dma((2, NY - 1)), dma((2, NY - 1)), dma((2, NX - 1)), dma((2, NZ - 1)), dma((2, NZ - 1)), dma((2, NY - 1)), dma((2, NY)),
        ],
        compiler_params=pltpu.CompilerParams(collective_id=1, has_side_effects=True, vmem_limit_bytes=24 << 20),
        name="projection_sum",
    )(partial.reshape(NX, TWIDE, Q))


def shards(points, pivots, targets):
    piv, own, tgt = gather_call(pivots, points, targets)
    factor, partial = factor_call(piv, own, tgt)
    return factor, reduce_call(partial).T


def solution(mesh):
    return jax.shard_map(
        shards,
        mesh=mesh,
        in_specs=(P("rows", "cols"), P(), P("rows", "cols")),
        out_specs=(P(("rows", "cols"), None), P(None, "cols")),
        check_vma=False,
    )
```

```python
import functools

import jax
import jax.numpy as jnp
from jax import lax
from jax.experimental import pallas as pl
from jax.experimental.pallas import tpu as pltpu
from jax.sharding import PartitionSpec as P

F32, BF16 = jnp.float32, jnp.bfloat16
MESH = pl.DeviceIdType.MESH
VMEM = pltpu.VMEM

HI = lax.Precision.HIGHEST
NT = (((1,), (1,)), ((), ()))
SUB, BLK, NB = 8, 128, 8
Q = NB * BLK
OWN = 256
RIDGE = 0.001
NZ, NY, NX = 8, 4, 4
E, TGT, LOCAL = 1024, 256, 1024
WIDE, TWIDE = E // NX, TGT // NX


def lanes(x, c):
    return jnp.broadcast_to(x[:, c:c + 1], (SUB, BLK))


def sublanes(x, s):
    return jnp.broadcast_to(x[s:s + 1, :], (SUB, BLK))


def small_factor(e):
    low, inv = {}, [None] * SUB
    for k in range(0, SUB, 2):
        a, b, c = e[k, k], e[k + 1, k], e[k + 1, k + 1]
        ra, rd = lax.rsqrt(a), lax.rsqrt(a * c - b * b)
        inv[k], inv[k + 1] = ra, a * ra * rd
        low[k + 1, k] = b * ra
        f = ra * rd
        for m in range(k + 2, SUB):
            low[m, k] = e[m, k] * ra
            low[m, k + 1] = (a * e[m, k + 1] - b * e[m, k]) * f
        for n in range(k + 2, SUB):
            for m in range(n, SUB):
                e[m, n] = e[m, n] - low[m, k] * low[n, k] - low[m, k + 1] * low[n, k + 1]
    return low, inv


def chol_inverse(a, emit, side, midway):
    groups = BLK // SUB
    lane = lax.broadcasted_iota(jnp.int32, (SUB, BLK), 1)
    sub = lax.broadcasted_iota(jnp.int32, (SUB, BLK), 0)
    w = [jnp.where(lane == sub + SUB * g, 1.0, 0.0).astype(F32) for g in range(groups)]
    side = list(side)
    for g in range(groups):
        cols = [lanes(a[g], SUB * g + k) for k in range(SUB)]
        low, inv = small_factor({(m, k): sublanes(cols[k], m) for k in range(SUB) for m in range(k, SUB)})
        us, ws = [], []
        for k in range(SUB):
            u, x = sublanes(a[g], k), sublanes(w[g], k)
            for j in range(k):
                u, x = u - us[j] * low[k, j], x - ws[j] * low[k, j]
            us.append(u * inv[k])
            ws.append(x * inv[k])
            emit(SUB * g + k, ws[k])
        for i in range(g + 1, groups):
            vs = []
            for k in range(SUB):
                v = lanes(a[i], SUB * g + k)
                for j in range(k):
                    v = v - vs[j] * low[k, j]
                vs.append(v * inv[k])
            ai, wi = a[i], w[i]
            for k in range(SUB):
                ai, wi = ai - vs[k] * us[k], wi - vs[k] * ws[k]
            a[i], w[i] = ai, wi
        take = -(-len(side) // (groups - g))
        for job in side[:take]:
            job()
        side = side[take:]
        if g == groups // 2 - 1:
            midway()


def dot_nt(a, b, precision=HI):
    return lax.dot_general(a, b, NT, precision=precision, preferred_element_type=F32)


def split(x):
    hi = x.astype(BF16)
    return hi, (x - hi.astype(F32)).astype(BF16)


def dot3(ah, al, bh, bl):
    d = functools.partial(lax.dot_general, dimension_numbers=NT, preferred_element_type=F32)
    return d(ah, bh) + (d(ah, bl) + d(al, bh))


def cuts(lo, hi, step):
    return [(s, min(s + step, hi)) for s in range(lo, hi, step)]


TP = TWIDE // 2
LHALF = Q // 2


def projection_sum(part_ref, m_ref, out_ref, inbox, sems):
    core_in, ax_in, by_in, ay_in, bx_in, z_in = inbox
    core_sem, ax_sem, by_sem, ay_sem, bx_sem, z_sem, gz_sem, gy_sem, gc_sem = sems
    row, x = lax.axis_index("rows"), lax.axis_index("cols")
    core, y, z = row % 2, (row // 2) % NY, row // (2 * NY)

    def at(z_, y_, core_, x_):
        return ((z_ * NY + y_) * 2 + core_, x_)

    sibling = at(z, y, 1 - core, x)
    xs = [(x + d) % NX for d in range(1, NX)]
    ys = [(y + d) % NY for d in range(1, NY)]
    zs = [(z + d) % NZ for d in range(1, NZ)]
    to_x = [at(z, y, core, v) for v in xs]
    to_y = [at(z, v, core, x) for v in ys]
    to_z = [at(v, y, core, x) for v in zs]
    barrier = pltpu.get_barrier_semaphore()
    peers = [sibling] + to_x + to_y + to_z
    for peer in peers:
        pl.semaphore_signal(barrier, inc=1, device_id=peer, device_id_type=MESH)
    pl.semaphore_wait(barrier, len(peers))
    started, flying = [], []

    def send(src, dst, sem, peer):
        c = pltpu.make_async_remote_copy(src_ref=src, dst_ref=dst, send_sem=sem.at[0], recv_sem=sem.at[1], device_id=peer, device_id_type=MESH)
        c.start()
        started.append(c)
        flying.append(c)

    def arrive():
        for c in flying:
            c.wait_recv()
        flying.clear()

    def lanes_of(c_, y_):
        return pl.ds(pl.multiple_of(c_ * LHALF + y_ * BLK, BLK), BLK)

    def half(c_):
        return pl.ds(pl.multiple_of(c_ * LHALF, LHALF), LHALF)

    def eight(v):
        return pl.ds(pl.multiple_of(v * SUB, SUB), SUB)

    every, first, second = pl.ds(0, NX), pl.ds(0, TP), pl.ds(TP, TP)
    mine, tile = half(core), lanes_of(core, y)

    def over_cores():
        send(part_ref.at[:, :, half(1 - core)], core_in, core_sem, sibling)

    def over_x_and_y():
        arrive()
        m_ref[:, :, mine] = part_ref[:, :, mine] + core_in[...]
        for d in range(NX - 1):
            send(m_ref.at[xs[d], first, mine], ax_in.at[d], ax_sem.at[:, d], to_x[d])
        for d in range(NY - 1):
            send(m_ref.at[every, second, lanes_of(core, ys[d])], by_in.at[d], by_sem.at[:, d], to_y[d])

    def over_y_and_x():
        arrive()
        m_ref[x, first, mine] = m_ref[x, first, mine] + ax_in[0] + ax_in[1] + ax_in[2]
        m_ref[every, second, tile] = m_ref[every, second, tile] + by_in[0] + by_in[1] + by_in[2]
        for d in range(NY - 1):
            send(m_ref.at[x, first, lanes_of(core, ys[d])], ay_in.at[d], ay_sem.at[:, d], to_y[d])
        for d in range(NX - 1):
            send(m_ref.at[xs[d], second, tile], bx_in.at[d], bx_sem.at[:, d], to_x[d])

    def over_z():
        arrive()
        m_ref[x, first, tile] = m_ref[x, first, tile] + ay_in[0] + ay_in[1] + ay_in[2]
        m_ref[x, second, tile] = m_ref[x, second, tile] + bx_in[0] + bx_in[1] + bx_in[2]
        for d in range(NZ - 1):
            send(m_ref.at[x, eight(zs[d]), tile], z_in.at[d], z_sem.at[:, d], to_z[d])

    def back_over_z():
        arrive()
        total = m_ref[x, eight(z), tile]
        for d in range(NZ - 1):
            total = total + z_in[d]
        out_ref[eight(z), tile] = total * (1.0 / 256.0)
        for d in range(NZ - 1):
            send(out_ref.at[eight(z), tile], out_ref.at[eight(z), tile], gz_sem.at[:, d], to_z[d])

    def back_over_y():
        arrive()
        for d in range(NY - 1):
            send(out_ref.at[:, tile], out_ref.at[:, tile], gy_sem.at[:, d], to_y[d])

    def back_over_cores():
        arrive()
        send(out_ref.at[:, mine], out_ref.at[:, mine], gc_sem, sibling)

    def finish():
        for c in started:
            c.wait_send()

    return over_cores, over_x_and_y, over_y_and_x, over_z, back_over_z, back_over_y, back_over_cores, arrive, finish


def factor_kernel(
    piv_hbm, own_hbm, tgt_hbm, fac_ref, proj_ref,
    x_ref, t_ref, hi_ref, lo_ref, low_ref, winv_ref, s_ref, col_ref, row_ref, diag_ref, kown_ref, load_sems,
    part_ref, m_ref, moment_ref, *rest,
):
    loads = [pltpu.make_async_copy(piv_hbm.at[b * BLK:(b + 1) * BLK, :], x_ref.at[b * BLK:(b + 1) * BLK, :], load_sems.at[b]) for b in range(NB)]
    loads.append(pltpu.make_async_copy(own_hbm, x_ref.at[Q:Q + OWN, :], load_sems.at[NB]))
    loads.append(pltpu.make_async_copy(tgt_hbm, t_ref, load_sems.at[NB + 1]))
    for c in loads:
        c.start()
    summing = projection_sum(part_ref, m_ref, moment_ref, rest[:6], rest[6:])

    def prepare(b):
        loads[b].wait()
        for r0, r1 in cuts(b * BLK, (b + 1) * BLK if b < NB else Q + OWN, BLK):
            v = x_ref[r0:r1, :]
            hi_ref[r0:r1, :], lo_ref[r0:r1, :] = split(v)
            norms = jnp.broadcast_to(jnp.sum(v * v, axis=1, keepdims=True), (BLK, BLK))
            col_ref[r0:r1, :] = norms
            if b < NB:
                row_ref[:, r0:r1] = jnp.transpose(norms)[0:SUB, :]

    def kern(r0, r1, c0, c1):
        cross = dot3(hi_ref[r0:r1, :], lo_ref[r0:r1, :], hi_ref[c0:c1, :], lo_ref[c0:c1, :])
        col = jnp.tile(col_ref[r0:r1, :], (1, (c1 - c0) // BLK))
        return jnp.exp((col + row_ref[0:1, c0:c1] - 2.0 * cross) * (-0.5 / E))

    def own_rows(c0, c1):
        kown_ref[:, c0:c1] = kern(Q, Q + OWN, c0, c1)

    def own_moment(c):
        if c == 0:
            loads[NB + 1].wait()
        part_ref[c] = lax.dot_general(
            t_ref[c], kown_ref[...], (((0,), (0,)), ((), ())), precision=HI, preferred_element_type=F32)

    def schur(r0, r1, k):
        c0, c1 = k * BLK, (k + 1) * BLK
        own = r0 >= Q
        v = kown_ref[:, c0:c1] if own else kern(r0, r1, c0, c1)
        if k > 0:
            v = v - dot_nt(fac_ref[:, 0:c0] if own else low_ref[r0:r1, 0:c0], low_ref[c0:c1, 0:c0])
        s_ref[k % 2, r0:r1, :] = v

    def panel(r0, r1, k):
        c0, c1 = k * BLK, (k + 1) * BLK
        v = dot_nt(s_ref[k % 2, r0:r1, :], winv_ref[k])
        if r0 < Q:
            low_ref[r0:r1, c0:c1] = v
        else:
            fac_ref[:, c0:c1] = v

    def project(k):
        c0, c1 = k * BLK, (k + 1) * BLK
        v = moment_ref[:, c0:c1]
        if k > 0:
            v = v - dot_nt(proj_ref[:, 0:c0], low_ref[c0:c1, 0:c0])
        proj_ref[:, c0:c1] = dot_nt(v, winv_ref[k])

    rows, columns = (lax.broadcasted_iota(jnp.int32, (BLK, BLK), d) for d in (0, 1))
    ridge = jnp.where(rows == columns, RIDGE, 0.0).astype(F32)

    def next_diagonal(k):
        r0, r1 = (k + 1) * BLK, (k + 2) * BLK
        v = kern(r0, r1, r0, r1) + ridge
        if k > 0:
            old = low_ref[r0:r1, 0:k * BLK]
            v = v - dot_nt(old, old)
        s_ref[k % 2, k * BLK:(k + 1) * BLK, :] = v

    def nothing():
        pass

    do = functools.partial
    midway = {1: summing[1], 2: summing[2], 3: summing[4], 4: summing[6]}
    at_end = {0: summing[0], 2: summing[3], 3: summing[5], 4: summing[7]}
    solving = {5: [0, 1], 6: [2, 3, 4], 7: [5, 6]}
    prepare(0)
    diag_ref[...] = kern(0, BLK, 0, BLK) + ridge
    for k in range(NB):
        c0, c1, c2 = k * BLK, (k + 1) * BLK, (k + 2) * BLK
        side = []
        if k == 0:
            side += [do(prepare, b) for b in range(1, NB + 1)]
            side += [do(own_rows, a, b) for a, b in cuts(0, Q, 256)]
            side += [do(own_moment, c) for c in range(NX)]
        spans = ([(c1, c2)] if k + 1 < NB else []) + cuts(c2, Q, 256) + [(Q, Q + OWN)]
        for r0, r1 in spans:
            if k > 0:
                side.append(do(panel, r0, r1, k - 1))
            side.append(do(schur, r0, r1, k))
            if r0 == c1 and r0 < Q:
                side.append(do(next_diagonal, k))
        side += [do(project, b) for b in solving.get(k, [])]

        def emit(row, value, k=k):
            winv_ref[k, row:row + 1, :] = value[0:1, :]

        chol_inverse([diag_ref[SUB * g:SUB * (g + 1), :] for g in range(BLK // SUB)], emit, side, midway.get(k, nothing))
        if k + 1 < NB:
            panel(c1, c2, k)
            last = low_ref[c1:c2, c0:c1]
            diag_ref[...] = s_ref[k % 2, c0:c1, :] - dot_nt(last, last)
        at_end.get(k, nothing)()
    panel(Q, Q + OWN, NB - 1)
    project(NB - 1)
    summing[8]()


def factor_call(piv, own, tgt):
    rows = Q + OWN
    dma = pltpu.SemaphoreType.DMA
    return pl.pallas_call(
        factor_kernel,
        out_shape=(jax.ShapeDtypeStruct((OWN, Q), F32), jax.ShapeDtypeStruct((TWIDE, Q), F32)),
        in_specs=[pl.BlockSpec(memory_space=pl.ANY)] * 3,
        out_specs=[pl.BlockSpec(memory_space=VMEM)] * 2,
        scratch_shapes=[
            VMEM((rows, E), F32), VMEM((NX, OWN, TWIDE), F32), VMEM((rows, E), BF16), VMEM((rows, E), BF16),
            VMEM((Q, Q), F32), VMEM((NB, BLK, BLK), F32), VMEM((2, rows, BLK), F32), VMEM((rows, BLK), F32), VMEM((SUB, Q), F32),
            VMEM((BLK, BLK), F32), VMEM((OWN, Q), F32), dma((NB + 2,)),
            VMEM((NX, TWIDE, Q), F32), VMEM((NX, TWIDE, Q), F32), VMEM((TWIDE, Q), F32),
            VMEM((NX, TWIDE, LHALF), F32), VMEM((NX - 1, TP, LHALF), F32), VMEM((NY - 1, NX, TP, BLK), F32),
            VMEM((NY - 1, TP, BLK), F32), VMEM((NX - 1, TP, BLK), F32), VMEM((NZ - 1, SUB, BLK), F32),
            dma((2,)), dma((2, NX - 1)), dma((2, NY - 1)), dma((2, NY - 1)), dma((2, NX - 1)), dma((2, NZ - 1)), dma((2, NZ - 1)), dma((2, NY - 1)), dma((2,)),
        ],
        compiler_params=pltpu.CompilerParams(collective_id=1, has_side_effects=True, vmem_limit_bytes=48 << 20),
        name="factor",
    )(piv, own, tgt)


HALF, YPART, ZPART = Q // 2, Q // 2 // NY, Q // 2 // NY // NZ
MID = YPART // 2


def picked_rows(ids_ref, points_ref, base, out_ref):
    x = points_ref[...]
    hi = x.astype(BF16)
    rest = x - hi.astype(F32)
    mid = rest.astype(BF16)
    low = (rest - mid.astype(F32)).astype(BF16)
    per_row = ids_ref.shape[1] // BLK
    spot = lax.broadcasted_iota(jnp.int32, (BLK, LOCAL), 1).astype(F32) + base.astype(F32)
    for b in range(NB):
        ids = ids_ref[b // per_row:b // per_row + 1, (b % per_row) * BLK:(b % per_row + 1) * BLK]
        column = jnp.transpose(jnp.broadcast_to(ids.astype(F32), (BLK, BLK)))
        hot = jnp.where(jnp.tile(column, (1, LOCAL // BLK)) == spot, 1.0, 0.0).astype(BF16)
        d = functools.partial(jnp.dot, preferred_element_type=F32)
        out_ref[b * BLK:(b + 1) * BLK, :] = (d(hot, hi) + d(hot, mid)) + d(hot, low)


def gather_kernel(
    ids_ref, points_ref, targets_ref, full_ref, own_ref, tgt_ref,
    pick, from_core, from_y, from_z, own_send, own_recv, tgt_send, tgt_recv,
    core_send, core_recv, y_send, y_recv, z_send, z_recv,
    gz_send, gz_recv, a1_send, a1_recv, b1_send, b1_recv, a2_send, a2_recv, b2_send, b2_recv, fwd_send, fwd_recv,
):
    row, x = lax.axis_index("rows"), lax.axis_index("cols")
    core, y, z = row % 2, (row // 2) % NY, row // (2 * NY)

    def at(z_, y_, core_, x_):
        return ((z_ * NY + y_) * 2 + core_, x_)

    sibling = at(z, y, 1 - core, x)
    xs = [(x + d) % NX for d in range(1, NX)]
    ys = [(y + d) % NY for d in range(1, NY)]
    zs = [(z + d) % NZ for d in range(1, NZ)]
    peers = [sibling] + [at(z, y, core, v) for v in xs] + [at(z, v, core, x) for v in ys] + [at(v, y, core, x) for v in zs]
    barrier = pltpu.get_barrier_semaphore()
    for peer in peers:
        pl.semaphore_signal(barrier, inc=1, device_id=peer, device_id_type=MESH)
    pl.semaphore_wait(barrier, len(peers))

    def send(src, dst, ssem, rsem, peer):
        c = pltpu.make_async_remote_copy(src_ref=src, dst_ref=dst, send_sem=ssem, recv_sem=rsem, device_id=peer, device_id_type=MESH)
        c.start()
        return c

    def part(i, n):
        return pl.ds(pl.multiple_of(i * n, n), n)

    moved = []
    for d, v in enumerate(xs):
        moved.append(send(points_ref.at[part(v, LOCAL // NX), :], own_ref.at[:, part(x, WIDE)], own_send.at[d], own_recv.at[d], at(z, y, core, v)))
        moved.append(send(targets_ref.at[part(v, LOCAL // NX), :], tgt_ref.at[x], tgt_send.at[d], tgt_recv.at[d], at(z, y, core, v)))
    own_ref[:, part(x, WIDE)] = points_ref[part(x, LOCAL // NX), :]
    tgt_ref[x] = targets_ref[part(x, LOCAL // NX), :]

    picked_rows(ids_ref, points_ref, row * LOCAL, pick)

    c = send(pick.at[part(1 - core, HALF), :], from_core, core_send, core_recv, sibling)
    c.wait_recv()
    mine = part(core, HALF)
    pick[mine, :] = pick[mine, :] + from_core[...]
    ysent = []
    for d, v in enumerate(ys):
        ysent.append(send(pick.at[pl.ds(pl.multiple_of(core * HALF + v * YPART, YPART), YPART), :], from_y.at[d], y_send.at[d], y_recv.at[d], at(z, v, core, x)))
    for s in ysent:
        s.wait_recv()
    at_y = pl.multiple_of(core * HALF + y * YPART, YPART)
    pick[pl.ds(at_y, YPART), :] = pick[pl.ds(at_y, YPART), :] + from_y[0] + from_y[1] + from_y[2]
    zsent = []
    for d, v in enumerate(zs):
        zsent.append(send(pick.at[pl.ds(pl.multiple_of(at_y + v * ZPART, ZPART), ZPART), :], from_z.at[d], z_send.at[d], z_recv.at[d], at(v, y, core, x)))
    for s in zsent:
        s.wait_recv()
    at_z = pl.multiple_of(at_y + z * ZPART, ZPART)
    total = pick[pl.ds(at_z, ZPART), :]
    for d in range(NZ - 1):
        total = total + from_z[d]
    cols_me = part(x, WIDE)
    full_ref[pl.ds(at_z, ZPART), cols_me] = total

    gz = [send(full_ref.at[pl.ds(at_z, ZPART), cols_me], full_ref.at[pl.ds(at_z, ZPART), cols_me], gz_send.at[d], gz_recv.at[d], at(v, y, core, x)) for d, v in enumerate(zs)]
    for s in gz:
        s.wait_recv()
    count = 0
    forwards = []

    def forward(rows, cols):
        k = len(forwards)
        forwards.append(send(full_ref.at[rows, cols], full_ref.at[rows, cols], fwd_send.at[k], fwd_recv.at[k], sibling))

    def rows_a(v):
        return pl.ds(pl.multiple_of(core * HALF + v * YPART, MID), MID)

    def rows_b(v):
        return pl.ds(pl.multiple_of(core * HALF + v * YPART + MID, MID), MID)

    everything = pl.ds(0, E)
    a1 = [send(full_ref.at[rows_a(y), cols_me], full_ref.at[rows_a(y), cols_me], a1_send.at[d], a1_recv.at[d], at(z, y, core, v)) for d, v in enumerate(xs)]
    b1 = [send(full_ref.at[rows_b(y), cols_me], full_ref.at[rows_b(y), cols_me], b1_send.at[d], b1_recv.at[d], at(z, v, core, x)) for d, v in enumerate(ys)]
    for s in a1:
        s.wait_recv()
    a2 = [send(full_ref.at[rows_a(y), everything], full_ref.at[rows_a(y), everything], a2_send.at[d], a2_recv.at[d], at(z, v, core, x)) for d, v in enumerate(ys)]
    forward(rows_a(y), everything)
    for s in b1:
        s.wait_recv()
    b2 = []
    for d, v in enumerate(xs):
        for u in range(NY):
            b2.append(send(full_ref.at[rows_b(u), cols_me], full_ref.at[rows_b(u), cols_me], b2_send.at[d, u], b2_recv.at[d, u], at(z, y, core, v)))
    for u in range(NY):
        forward(rows_b(u), cols_me)
    for d in range(NY - 1):
        a2[d].wait_recv()
        forward(rows_a((y + NY - 1 - d) % NY), everything)
    for d in range(NX - 1):
        for u in range(NY):
            b2[d * NY + u].wait_recv()
            forward(rows_b(u), part((x + NX - 1 - d) % NX, WIDE))
    for s in forwards:
        s.wait_recv()
    for s in moved:
        s.wait_recv()
    for s in moved + [c] + ysent + zsent + gz + a1 + b1 + a2 + b2 + forwards:
        s.wait_send()


def gather_call(pivots, points, targets):
    dma = pltpu.SemaphoreType.DMA
    n_fwd = 1 + NY + (NY - 1) + (NX - 1) * NY
    return pl.pallas_call(
        gather_kernel,
        out_shape=(
            jax.ShapeDtypeStruct((Q, E), F32),
            jax.ShapeDtypeStruct((OWN, E), F32),
            jax.ShapeDtypeStruct((NX, OWN, TWIDE), F32),
        ),
        in_specs=[pl.BlockSpec(memory_space=VMEM)] * 3,
        out_specs=[pl.BlockSpec(memory_space=VMEM)] * 3,
        scratch_shapes=[
            VMEM((Q, WIDE), F32), VMEM((HALF, WIDE), F32), VMEM((NY - 1, YPART, WIDE), F32), VMEM((NZ - 1, ZPART, WIDE), F32),
            dma((NX - 1,)), dma((NX - 1,)), dma((NX - 1,)), dma((NX - 1,)),
            dma, dma, dma((NY - 1,)), dma((NY - 1,)), dma((NZ - 1,)), dma((NZ - 1,)),
            dma((NZ - 1,)), dma((NZ - 1,)), dma((NX - 1,)), dma((NX - 1,)), dma((NY - 1,)), dma((NY - 1,)),
            dma((NY - 1,)), dma((NY - 1,)), dma((NX - 1, NY)), dma((NX - 1, NY)), dma((n_fwd,)), dma((n_fwd,)),
        ],
        compiler_params=pltpu.CompilerParams(collective_id=0, has_side_effects=True, vmem_limit_bytes=40 << 20),
        name="pivot_gather",
    )(pivots, points, targets)


def shards(points, pivots, targets):
    factor, projection = factor_call(*gather_call(pivots, points, targets))
    return factor, projection.T


def solution(mesh):
    return jax.shard_map(
        shards,
        mesh=mesh,
        in_specs=(P("rows", "cols"), P(), P("rows", "cols")),
        out_specs=(P(("rows", "cols"), None), P(None, "cols")),
        check_vma=False,
    )
```

```python
import functools

import jax
import jax.numpy as jnp
from jax import lax
from jax.experimental import pallas as pl
from jax.experimental.pallas import tpu as pltpu
from jax.sharding import PartitionSpec as P

F32, BF16 = jnp.float32, jnp.bfloat16
MESH = pl.DeviceIdType.MESH
VMEM = pltpu.VMEM

HI = lax.Precision.HIGHEST
NT = (((1,), (1,)), ((), ()))
SUB, BLK, NB = 8, 128, 8
Q = NB * BLK
OWN = 256
RIDGE = 0.001
NZ, NY, NX = 8, 4, 4
E, TGT, LOCAL = 1024, 256, 1024
WIDE, TWIDE = E // NX, TGT // NX


def lanes(x, c):
    return jnp.broadcast_to(x[:, c:c + 1], (SUB, BLK))


def sublanes(x, s):
    return jnp.broadcast_to(x[s:s + 1, :], (SUB, BLK))


def small_factor(e):
    low, inv = {}, [None] * SUB
    for k in range(0, SUB, 2):
        a, b, c = e[k, k], e[k + 1, k], e[k + 1, k + 1]
        ra, rd = lax.rsqrt(a), lax.rsqrt(a * c - b * b)
        inv[k], inv[k + 1] = ra, a * ra * rd
        low[k + 1, k] = b * ra
        f = ra * rd
        for m in range(k + 2, SUB):
            low[m, k] = e[m, k] * ra
            low[m, k + 1] = (a * e[m, k + 1] - b * e[m, k]) * f
        for n in range(k + 2, SUB):
            for m in range(n, SUB):
                e[m, n] = e[m, n] - low[m, k] * low[n, k] - low[m, k + 1] * low[n, k + 1]
    return low, inv


def chol_inverse(a, emit, side, midway, late):
    groups = BLK // SUB
    lane = lax.broadcasted_iota(jnp.int32, (SUB, BLK), 1)
    sub = lax.broadcasted_iota(jnp.int32, (SUB, BLK), 0)
    w = [jnp.where(lane == sub + SUB * g, 1.0, 0.0).astype(F32) for g in range(groups)]
    side = list(side)
    for g in range(groups):
        cols = [lanes(a[g], SUB * g + k) for k in range(SUB)]
        low, inv = small_factor({(m, k): sublanes(cols[k], m) for k in range(SUB) for m in range(k, SUB)})
        us, ws = [], []
        for k in range(SUB):
            u, x = sublanes(a[g], k), sublanes(w[g], k)
            for j in range(k):
                u, x = u - us[j] * low[k, j], x - ws[j] * low[k, j]
            us.append(u * inv[k])
            ws.append(x * inv[k])
            emit(SUB * g + k, ws[k])
        for i in range(g + 1, groups):
            vs = []
            for k in range(SUB):
                v = lanes(a[i], SUB * g + k)
                for j in range(k):
                    v = v - vs[j] * low[k, j]
                vs.append(v * inv[k])
            ai, wi = a[i], w[i]
            for k in range(SUB):
                ai, wi = ai - vs[k] * us[k], wi - vs[k] * ws[k]
            a[i], w[i] = ai, wi
        take = 0 if late and g < groups // 2 else -(-len(side) // (groups - g))
        for job in side[:take]:
            job()
        side = side[take:]
        if g == groups // 2 - 1:
            midway()


def dot_nt(a, b, precision=HI):
    return lax.dot_general(a, b, NT, precision=precision, preferred_element_type=F32)


def split(x):
    hi = x.astype(BF16)
    return hi, (x - hi.astype(F32)).astype(BF16)


def dot3(ah, al, bh, bl):
    d = functools.partial(lax.dot_general, dimension_numbers=NT, preferred_element_type=F32)
    return d(ah, bh) + (d(ah, bl) + d(al, bh))


def cuts(lo, hi, step):
    return [(s, min(s + step, hi)) for s in range(lo, hi, step)]


TP = TWIDE // 2
ROWS = Q // (2 * NY * NZ)
LHALF = Q // 2


def neighbours():
    row, x = lax.axis_index("rows"), lax.axis_index("cols")
    core, y, z = row % 2, (row // 2) % NY, row // (2 * NY)

    def at(z_, y_, core_, x_):
        return ((z_ * NY + y_) * 2 + core_, x_)

    xs = [(x + d) % NX for d in range(1, NX)]
    ys = [(y + d) % NY for d in range(1, NY)]
    zs = [(z + d) % NZ for d in range(1, NZ)]
    sibling = at(z, y, 1 - core, x)
    to_x = [at(z, y, core, v) for v in xs]
    to_y = [at(z, v, core, x) for v in ys]
    to_z = [at(v, y, core, x) for v in zs]
    barrier = pltpu.get_barrier_semaphore()
    peers = [sibling] + to_x + to_y + to_z
    for peer in peers:
        pl.semaphore_signal(barrier, inc=1, device_id=peer, device_id_type=MESH)
    pl.semaphore_wait(barrier, len(peers))
    return (row, core, x, y, z), (xs, ys, zs), (sibling, to_x, to_y, to_z)


class Flights:
    def __init__(self):
        self.started = []

    def send(self, src, dst, sem, peer):
        c = pltpu.make_async_remote_copy(src_ref=src, dst_ref=dst, send_sem=sem.at[0], recv_sem=sem.at[1], device_id=peer, device_id_type=MESH)
        c.start()
        self.started.append(c)
        return c


def arrived(copies):
    for c in copies:
        c.wait_recv()


def picked_rows(ids_ref, points_ref, base, out_ref):
    x = points_ref[...]
    hi = x.astype(BF16)
    rest = x - hi.astype(F32)
    mid = rest.astype(BF16)
    low = (rest - mid.astype(F32)).astype(BF16)
    per_row = ids_ref.shape[1] // BLK
    spot = lax.broadcasted_iota(jnp.int32, (BLK, LOCAL), 1).astype(F32) + base.astype(F32)
    for b in range(NB):
        ids = ids_ref[b // per_row:b // per_row + 1, (b % per_row) * BLK:(b % per_row + 1) * BLK]
        column = jnp.transpose(jnp.broadcast_to(ids.astype(F32), (BLK, BLK)))
        hot = jnp.where(jnp.tile(column, (1, LOCAL // BLK)) == spot, 1.0, 0.0).astype(BF16)
        d = functools.partial(jnp.dot, preferred_element_type=F32)
        out_ref[b] = ((d(hot, hi) + d(hot, mid)) + d(hot, low)).reshape(2, NY, ROWS, WIDE)


def gather_pivots(flights, place, others, to, ids_ref, points_ref, targets_ref, xq_ref, own_ref, t_ref, pick, inbox, sems):
    (row, core, x, y, z), (xs, ys, zs), (sibling, to_x, to_y, to_z) = place, others, to
    from_core, from_y, from_z = inbox
    own_sem, tgt_sem, core_sem, y_sem, z_sem, gz_sem, a1_sem, b1_sem, a2_sem, b2_sem, fwd_sem = sems
    send = flights.send
    cols = pl.ds(pl.multiple_of(x * WIDE, WIDE), WIDE)

    def quarter(v):
        return pl.ds(pl.multiple_of(v * OWN, OWN), OWN)

    moved = []
    for d, v in enumerate(xs):
        moved.append(send(points_ref.at[quarter(v), :], own_ref.at[:, cols], own_sem.at[:, d], to_x[d]))
        moved.append(send(targets_ref.at[quarter(v), :], t_ref.at[x], tgt_sem.at[:, d], to_x[d]))
    own_ref[:, cols] = points_ref[quarter(x), :]
    t_ref[x] = targets_ref[quarter(x), :]
    picked_rows(ids_ref, points_ref, row * LOCAL, pick)

    arrived([send(pick.at[:, 1 - core], from_core, core_sem, sibling)])
    pick[:, core] = pick[:, core] + from_core[...]
    arrived([send(pick.at[:, core, ys[d]], from_y.at[d], y_sem.at[:, d], to_y[d]) for d in range(NY - 1)])
    pick[:, core, y] = pick[:, core, y] + from_y[0] + from_y[1] + from_y[2]
    arrived([send(pick.at[zs[d], core, y], from_z.at[d], z_sem.at[:, d], to_z[d]) for d in range(NZ - 1)])
    total = pick[z, core, y]
    for d in range(NZ - 1):
        total = total + from_z[d]
    xq_ref[z, core, y, :, cols] = total

    def same(place_, sem, peer):
        return send(xq_ref.at[place_], xq_ref.at[place_], sem, peer)

    arrived([same((z, core, y, slice(None), cols), gz_sem.at[:, d], to_z[d]) for d in range(NZ - 1)])
    first, second = pl.ds(0, SUB), pl.ds(SUB, SUB)
    groups = (pl.ds(0, 2), pl.ds(2, NB - 2))
    step1, step2 = [], []
    for n, blocks in enumerate(groups):
        step1.append([same((blocks, core, y, first, cols), a1_sem.at[:, n, d], to_x[d]) for d in range(NX - 1)]
                     + [same((blocks, core, y, second, cols), b1_sem.at[:, n, d], to_y[d]) for d in range(NY - 1)])
    for n, blocks in enumerate(groups):
        arrived(step1[n])
        step2.append([same((blocks, core, y, first), a2_sem.at[:, n, d], to_y[d]) for d in range(NY - 1)]
                     + [same((blocks, core, slice(None), second, cols), b2_sem.at[:, n, d], to_x[d]) for d in range(NX - 1)])
    arrived(step2[0])
    arrived([same((groups[0], core), fwd_sem.at[:, 0], sibling)])
    late = []

    def forward():
        arrived(step2[1])
        late.append(same((groups[1], core), fwd_sem.at[:, 1], sibling))

    def rest():
        arrived(late + moved)

    return forward, rest


def projection_sum(flights, place, others, to, part_ref, m_ref, out_ref, inbox, sems):
    core_in, ax_in, by_in, ay_in, bx_in, z_in = inbox
    core_sem, ax_sem, by_sem, ay_sem, bx_sem, z_sem, gz_sem, gy_sem, gc_sem = sems
    (row, core, x, y, z), (xs, ys, zs), (sibling, to_x, to_y, to_z) = place, others, to
    flying = []

    def send(src, dst, sem, peer):
        flying.append(flights.send(src, dst, sem, peer))

    def arrive():
        arrived(flying)
        flying.clear()

    def lanes_of(c_, y_):
        return pl.ds(pl.multiple_of(c_ * LHALF + y_ * BLK, BLK), BLK)

    def half(c_):
        return pl.ds(pl.multiple_of(c_ * LHALF, LHALF), LHALF)

    def eight(v):
        return pl.ds(pl.multiple_of(v * SUB, SUB), SUB)

    every, first, second = pl.ds(0, NX), pl.ds(0, TP), pl.ds(TP, TP)
    mine, tile = half(core), lanes_of(core, y)

    def over_cores():
        send(part_ref.at[:, :, half(1 - core)], core_in, core_sem, sibling)

    def over_x_and_y():
        arrive()
        m_ref[:, :, mine] = part_ref[:, :, mine] + core_in[...]
        for d in range(NX - 1):
            send(m_ref.at[xs[d], first, mine], ax_in.at[d], ax_sem.at[:, d], to_x[d])
        for d in range(NY - 1):
            send(m_ref.at[every, second, lanes_of(core, ys[d])], by_in.at[d], by_sem.at[:, d], to_y[d])

    def over_y_and_x():
        arrive()
        m_ref[x, first, mine] = m_ref[x, first, mine] + ax_in[0] + ax_in[1] + ax_in[2]
        m_ref[every, second, tile] = m_ref[every, second, tile] + by_in[0] + by_in[1] + by_in[2]
        for d in range(NY - 1):
            send(m_ref.at[x, first, lanes_of(core, ys[d])], ay_in.at[d], ay_sem.at[:, d], to_y[d])
        for d in range(NX - 1):
            send(m_ref.at[xs[d], second, tile], bx_in.at[d], bx_sem.at[:, d], to_x[d])

    def over_z():
        arrive()
        m_ref[x, first, tile] = m_ref[x, first, tile] + ay_in[0] + ay_in[1] + ay_in[2]
        m_ref[x, second, tile] = m_ref[x, second, tile] + bx_in[0] + bx_in[1] + bx_in[2]
        for d in range(NZ - 1):
            send(m_ref.at[x, eight(zs[d]), tile], z_in.at[d], z_sem.at[:, d], to_z[d])

    def back_over_z():
        arrive()
        total = m_ref[x, eight(z), tile]
        for d in range(NZ - 1):
            total = total + z_in[d]
        out_ref[eight(z), tile] = total * (1.0 / 256.0)
        for d in range(NZ - 1):
            send(out_ref.at[eight(z), tile], out_ref.at[eight(z), tile], gz_sem.at[:, d], to_z[d])

    def back_over_y():
        arrive()
        for d in range(NY - 1):
            send(out_ref.at[:, tile], out_ref.at[:, tile], gy_sem.at[:, d], to_y[d])

    def back_over_cores():
        arrive()
        send(out_ref.at[:, mine], out_ref.at[:, mine], gc_sem, sibling)

    return over_cores, over_x_and_y, over_y_and_x, over_z, back_over_z, back_over_y, back_over_cores, arrive


def factor_kernel(
    ids_ref, points_ref, targets_ref, fac_ref, proj_ref,
    xq_ref, own_ref, t_ref, pick_ref, hi_ref, lo_ref, low_ref, winv_ref, s_ref, col_ref, row_ref, diag_ref, kown_ref,
    part_ref, m_ref, moment_ref, *rest,
):
    where = neighbours()
    flights = Flights()
    forward, arrive_rest = gather_pivots(
        flights, *where, ids_ref, points_ref, targets_ref, xq_ref, own_ref, t_ref, pick_ref, rest[:3], rest[3:14])
    summing = projection_sum(flights, *where, part_ref, m_ref, moment_ref, rest[14:20], rest[20:])

    def prepare(b):
        for r0, r1 in cuts(b * BLK, (b + 1) * BLK if b < NB else Q + OWN, BLK):
            v = xq_ref[b].reshape(BLK, E) if b < NB else own_ref[r0 - Q:r1 - Q, :]
            hi_ref[r0:r1, :], lo_ref[r0:r1, :] = split(v)
            norms = jnp.broadcast_to(jnp.sum(v * v, axis=1, keepdims=True), (BLK, BLK))
            col_ref[r0:r1, :] = norms
            if b < NB:
                row_ref[:, r0:r1] = jnp.transpose(norms)[0:SUB, :]

    def kern(r0, r1, c0, c1):
        cross = dot3(hi_ref[r0:r1, :], lo_ref[r0:r1, :], hi_ref[c0:c1, :], lo_ref[c0:c1, :])
        col = jnp.tile(col_ref[r0:r1, :], (1, (c1 - c0) // BLK))
        return jnp.exp((col + row_ref[0:1, c0:c1] - 2.0 * cross) * (-0.5 / E))

    def own_rows(c0, c1):
        kown_ref[:, c0:c1] = kern(Q, Q + OWN, c0, c1)

    def own_moment(c):
        part_ref[c] = lax.dot_general(
            t_ref[c], kown_ref[...], (((0,), (0,)), ((), ())), precision=HI, preferred_element_type=F32)

    def schur(r0, r1, k):
        c0, c1 = k * BLK, (k + 1) * BLK
        own = r0 >= Q
        v = kown_ref[:, c0:c1] if own else kern(r0, r1, c0, c1)
        if k > 0:
            v = v - dot_nt(fac_ref[:, 0:c0] if own else low_ref[r0:r1, 0:c0], low_ref[c0:c1, 0:c0])
        s_ref[k % 2, r0:r1, :] = v

    def panel(r0, r1, k):
        c0, c1 = k * BLK, (k + 1) * BLK
        v = dot_nt(s_ref[k % 2, r0:r1, :], winv_ref[k])
        if r0 < Q:
            low_ref[r0:r1, c0:c1] = v
        else:
            fac_ref[:, c0:c1] = v

    def project(k):
        c0, c1 = k * BLK, (k + 1) * BLK
        v = moment_ref[:, c0:c1]
        if k > 0:
            v = v - dot_nt(proj_ref[:, 0:c0], low_ref[c0:c1, 0:c0])
        proj_ref[:, c0:c1] = dot_nt(v, winv_ref[k])

    rows, columns = (lax.broadcasted_iota(jnp.int32, (BLK, BLK), d) for d in (0, 1))
    ridge = jnp.where(rows == columns, RIDGE, 0.0).astype(F32)

    def next_diagonal(k):
        r0, r1 = (k + 1) * BLK, (k + 2) * BLK
        v = kern(r0, r1, r0, r1) + ridge
        if k > 0:
            old = low_ref[r0:r1, 0:k * BLK]
            v = v - dot_nt(old, old)
        s_ref[k % 2, k * BLK:(k + 1) * BLK, :] = v

    def nothing():
        pass

    do = functools.partial
    midway = {1: arrive_rest, 3: summing[1], 4: summing[2], 5: summing[4], 6: summing[6]}
    at_end = {0: forward, 2: summing[0], 4: summing[3], 5: summing[5], 6: summing[7]}
    spans = [(b * BLK, (b + 1) * BLK) for b in range(NB)] + [(Q, Q + OWN)]
    columns_of = {span: 0 for span in spans}

    def advance(span, k):
        jobs = []
        while columns_of[span] <= k:
            c = columns_of[span]
            if c > 0:
                jobs.append(do(panel, *span, c - 1))
            jobs.append(do(schur, *span, c))
            columns_of[span] = c + 1
        return jobs

    prepare(0)
    diag_ref[...] = kern(0, BLK, 0, BLK) + ridge
    for k in range(NB):
        c0, c1, c2 = k * BLK, (k + 1) * BLK, (k + 2) * BLK
        early, side = [], []
        if k == 0:
            early.append(do(prepare, 1))
        if k == 1:
            side += [do(prepare, b) for b in range(2, NB + 1)]
        if k == 2:
            early += [do(own_rows, a, b) for a, b in cuts(0, Q, 256)]
            early += [do(own_moment, c) for c in range(NX)]
        if k + 1 < NB:
            side += advance(spans[k + 1], k) + [do(next_diagonal, k)]
        if k == 1:
            side = side[:1] + side[NB - 1:] + side[1:NB - 1]
        if k > 1:
            for span in spans[min(k + 2, NB):]:
                side += advance(span, k)
        if k == NB - 1:
            side += [do(project, b) for b in range(NB - 1)]
        if k == 2:
            side = side[:2 * (k + 1)] + early + side[2 * (k + 1):]
            early = []
        elif k == 0:
            side, early = early + side, []

        def emit(row, value, k=k):
            winv_ref[k, row:row + 1, :] = value[0:1, :]

        chol_inverse([diag_ref[SUB * g:SUB * (g + 1), :] for g in range(BLK // SUB)], emit, side, midway.get(k, nothing), k == 1)
        if k + 1 < NB:
            panel(c1, c2, k)
            last = low_ref[c1:c2, c0:c1]
            diag_ref[...] = s_ref[k % 2, c0:c1, :] - dot_nt(last, last)
        at_end.get(k, nothing)()
    panel(Q, Q + OWN, NB - 1)
    project(NB - 1)
    for c in flights.started:
        c.wait_send()


def factor_call(pivots, points, targets):
    rows = Q + OWN
    dma = pltpu.SemaphoreType.DMA
    return pl.pallas_call(
        factor_kernel,
        out_shape=(jax.ShapeDtypeStruct((OWN, Q), F32), jax.ShapeDtypeStruct((TWIDE, Q), F32)),
        in_specs=[pl.BlockSpec(memory_space=VMEM)] * 3,
        out_specs=[pl.BlockSpec(memory_space=VMEM)] * 2,
        scratch_shapes=[
            VMEM((NZ, 2, NY, ROWS, E), F32), VMEM((OWN, E), F32), VMEM((NX, OWN, TWIDE), F32), VMEM((NZ, 2, NY, ROWS, WIDE), F32),
            VMEM((rows, E), BF16), VMEM((rows, E), BF16), VMEM((Q, Q), F32), VMEM((NB, BLK, BLK), F32), VMEM((2, rows, BLK), F32),
            VMEM((rows, BLK), F32), VMEM((SUB, Q), F32), VMEM((BLK, BLK), F32), VMEM((OWN, Q), F32),
            VMEM((NX, TWIDE, Q), F32), VMEM((NX, TWIDE, Q), F32), VMEM((TWIDE, Q), F32),
            VMEM((NZ, NY, ROWS, WIDE), F32), VMEM((NY - 1, NZ, ROWS, WIDE), F32), VMEM((NZ - 1, ROWS, WIDE), F32),
            dma((2, NX - 1)), dma((2, NX - 1)), dma((2,)), dma((2, NY - 1)), dma((2, NZ - 1)), dma((2, NZ - 1)),
            dma((2, 2, NX - 1)), dma((2, 2, NY - 1)), dma((2, 2, NY - 1)), dma((2, 2, NX - 1)), dma((2, 2)),
            VMEM((NX, TWIDE, LHALF), F32), VMEM((NX - 1, TP, LHALF), F32), VMEM((NY - 1, NX, TP, BLK), F32),
            VMEM((NY - 1, TP, BLK), F32), VMEM((NX - 1, TP, BLK), F32), VMEM((NZ - 1, SUB, BLK), F32),
            dma((2,)), dma((2, NX - 1)), dma((2, NY - 1)), dma((2, NY - 1)), dma((2, NX - 1)), dma((2, NZ - 1)), dma((2, NZ - 1)), dma((2, NY - 1)), dma((2,)),
        ],
        compiler_params=pltpu.CompilerParams(collective_id=0, has_side_effects=True, vmem_limit_bytes=48 << 20),
        name="factor",
    )(pivots, points, targets)


def shards(points, pivots, targets):
    factor, projection = factor_call(pivots, points, targets)
    return factor, projection.T


def solution(mesh):
    return jax.shard_map(
        shards,
        mesh=mesh,
        in_specs=(P("rows", "cols"), P(), P("rows", "cols")),
        out_specs=(P(("rows", "cols"), None), P(None, "cols")),
        check_vma=False,
    )
```

```python
import functools

import jax
import jax.numpy as jnp
from jax import lax
from jax.experimental import pallas as pl
from jax.experimental.pallas import tpu as pltpu
from jax.sharding import PartitionSpec as P

F32, BF16 = jnp.float32, jnp.bfloat16
MESH = pl.DeviceIdType.MESH
VMEM = pltpu.VMEM

HI = lax.Precision.HIGHEST
NT = (((1,), (1,)), ((), ()))
SUB, BLK, NB = 8, 128, 8
Q = NB * BLK
OWN = 256
RIDGE = 0.001
NZ, NY, NX = 8, 4, 4
E, TGT, LOCAL = 1024, 256, 1024
WIDE, TWIDE = E // NX, TGT // NX


def lanes(x, c):
    return jnp.broadcast_to(x[:, c:c + 1], (SUB, BLK))


def sublanes(x, s):
    return jnp.broadcast_to(x[s:s + 1, :], (SUB, BLK))


def small_factor(e):
    low, inv = {}, [None] * SUB
    for k in range(0, SUB, 2):
        a, b, c = e[k, k], e[k + 1, k], e[k + 1, k + 1]
        ra, rd = lax.rsqrt(a), lax.rsqrt(a * c - b * b)
        inv[k], inv[k + 1] = ra, a * ra * rd
        low[k + 1, k] = b * ra
        f = ra * rd
        for m in range(k + 2, SUB):
            low[m, k] = e[m, k] * ra
            low[m, k + 1] = (a * e[m, k + 1] - b * e[m, k]) * f
        for n in range(k + 2, SUB):
            for m in range(n, SUB):
                e[m, n] = e[m, n] - low[m, k] * low[n, k] - low[m, k + 1] * low[n, k + 1]
    return low, inv


def chol_inverse(a, emit, side, midway, late):
    groups = BLK // SUB
    lane = lax.broadcasted_iota(jnp.int32, (SUB, BLK), 1)
    sub = lax.broadcasted_iota(jnp.int32, (SUB, BLK), 0)
    w = [jnp.where(lane == sub + SUB * g, 1.0, 0.0).astype(F32) for g in range(groups)]
    side = list(side)
    for g in range(groups):
        cols = [lanes(a[g], SUB * g + k) for k in range(SUB)]
        low, inv = small_factor({(m, k): sublanes(cols[k], m) for k in range(SUB) for m in range(k, SUB)})
        us, ws = [], []
        for k in range(SUB):
            u, x = sublanes(a[g], k), sublanes(w[g], k)
            for j in range(k):
                u, x = u - us[j] * low[k, j], x - ws[j] * low[k, j]
            us.append(u * inv[k])
            ws.append(x * inv[k])
            emit(SUB * g + k, ws[k])
        for i in range(g + 1, groups):
            vs = []
            for k in range(SUB):
                v = lanes(a[i], SUB * g + k)
                for j in range(k):
                    v = v - vs[j] * low[k, j]
                vs.append(v * inv[k])
            ai, wi = a[i], w[i]
            for k in range(SUB):
                ai, wi = ai - vs[k] * us[k], wi - vs[k] * ws[k]
            a[i], w[i] = ai, wi
        take = 0 if late and g < groups // 2 else -(-len(side) // (groups - g))
        for job in side[:take]:
            job()
        side = side[take:]
        if g == groups // 2 - 1:
            midway()


def dot_nt(a, b, precision=HI):
    return lax.dot_general(a, b, NT, precision=precision, preferred_element_type=F32)


def split(x):
    hi = x.astype(BF16)
    return hi, (x - hi.astype(F32)).astype(BF16)


def dot3(ah, al, bh, bl):
    d = functools.partial(lax.dot_general, dimension_numbers=NT, preferred_element_type=F32)
    return d(ah, bh) + (d(ah, bl) + d(al, bh))


def cuts(lo, hi, step):
    return [(s, min(s + step, hi)) for s in range(lo, hi, step)]


TP = TWIDE // 2
ROWS = Q // (2 * NY * NZ)
LHALF = Q // 2


def neighbours():
    row, x = lax.axis_index("rows"), lax.axis_index("cols")
    core, y, z = row % 2, (row // 2) % NY, row // (2 * NY)

    def at(z_, y_, core_, x_):
        return ((z_ * NY + y_) * 2 + core_, x_)

    xs = [(x + d) % NX for d in range(1, NX)]
    ys = [(y + d) % NY for d in range(1, NY)]
    zs = [(z + d) % NZ for d in range(1, NZ)]
    sibling = at(z, y, 1 - core, x)
    to_x = [at(z, y, core, v) for v in xs]
    to_y = [at(z, v, core, x) for v in ys]
    to_z = [at(v, y, core, x) for v in zs]
    barrier = pltpu.get_barrier_semaphore()
    peers = [sibling] + to_x + to_y + to_z
    for peer in peers:
        pl.semaphore_signal(barrier, inc=1, device_id=peer, device_id_type=MESH)
    pl.semaphore_wait(barrier, len(peers))
    return (row, core, x, y, z), (xs, ys, zs), (sibling, to_x, to_y, to_z)


class Flights:
    def __init__(self):
        self.started = []

    def send(self, src, dst, sem, peer):
        c = pltpu.make_async_remote_copy(src_ref=src, dst_ref=dst, send_sem=sem.at[0], recv_sem=sem.at[1], device_id=peer, device_id_type=MESH)
        c.start()
        self.started.append(c)
        return c


def arrived(copies):
    for c in copies:
        c.wait_recv()


def picked_rows(ids_ref, points_ref, base, out_ref):
    x = points_ref[...]
    hi = x.astype(BF16)
    rest = x - hi.astype(F32)
    mid = rest.astype(BF16)
    low = (rest - mid.astype(F32)).astype(BF16)
    per_row = ids_ref.shape[1] // BLK
    spot = lax.broadcasted_iota(jnp.int32, (BLK, LOCAL), 1).astype(F32) + base.astype(F32)
    for b in range(NB):
        ids = ids_ref[b // per_row:b // per_row + 1, (b % per_row) * BLK:(b % per_row + 1) * BLK]
        column = jnp.transpose(jnp.broadcast_to(ids.astype(F32), (BLK, BLK)))
        hot = jnp.where(jnp.tile(column, (1, LOCAL // BLK)) == spot, 1.0, 0.0).astype(BF16)
        d = functools.partial(jnp.dot, preferred_element_type=F32)
        out_ref[b] = ((d(hot, hi) + d(hot, mid)) + d(hot, low)).reshape(2, NY, ROWS, WIDE)


def gather_pivots(flights, place, others, to, ids_ref, points_ref, targets_ref, xq_ref, own_ref, t_ref, pick, inbox, sems):
    (row, core, x, y, z), (xs, ys, zs), (sibling, to_x, to_y, to_z) = place, others, to
    from_core, from_y, from_z = inbox
    own_sem, tgt_sem, core_sem, y_sem, z_sem, gz_sem, a1_sem, b1_sem, a2_sem, b2_sem, fwd_sem = sems
    send = flights.send
    cols = pl.ds(pl.multiple_of(x * WIDE, WIDE), WIDE)

    def quarter(v):
        return pl.ds(pl.multiple_of(v * OWN, OWN), OWN)

    moved = []
    for d, v in enumerate(xs):
        moved.append(send(points_ref.at[quarter(v), :], own_ref.at[:, cols], own_sem.at[:, d], to_x[d]))
        moved.append(send(targets_ref.at[:, quarter(v)], t_ref.at[x], tgt_sem.at[:, d], to_x[d]))
    own_ref[:, cols] = points_ref[quarter(x), :]
    t_ref[x] = targets_ref[:, quarter(x)]
    picked_rows(ids_ref, points_ref, row * LOCAL, pick)

    arrived([send(pick.at[:, 1 - core], from_core, core_sem, sibling)])
    pick[:, core] = pick[:, core] + from_core[...]
    arrived([send(pick.at[:, core, ys[d]], from_y.at[d], y_sem.at[:, d], to_y[d]) for d in range(NY - 1)])
    pick[:, core, y] = pick[:, core, y] + from_y[0] + from_y[1] + from_y[2]
    arrived([send(pick.at[zs[d], core, y], from_z.at[d], z_sem.at[:, d], to_z[d]) for d in range(NZ - 1)])
    total = pick[z, core, y]
    for d in range(NZ - 1):
        total = total + from_z[d]
    xq_ref[z, core, y, :, cols] = total

    def same(place_, sem, peer):
        return send(xq_ref.at[place_], xq_ref.at[place_], sem, peer)

    arrived([same((z, core, y, slice(None), cols), gz_sem.at[:, d], to_z[d]) for d in range(NZ - 1)])
    first, second = pl.ds(0, SUB), pl.ds(SUB, SUB)
    groups = (pl.ds(0, 2), pl.ds(2, 2), pl.ds(4, NB - 4))
    step1, step2 = [], []
    for n, blocks in enumerate(groups):
        step1.append([same((blocks, core, y, first, cols), a1_sem.at[:, n, d], to_x[d]) for d in range(NX - 1)]
                     + [same((blocks, core, y, second, cols), b1_sem.at[:, n, d], to_y[d]) for d in range(NY - 1)])
    for n, blocks in enumerate(groups):
        arrived(step1[n])
        step2.append([same((blocks, core, y, first), a2_sem.at[:, n, d], to_y[d]) for d in range(NY - 1)]
                     + [same((blocks, core, slice(None), second, cols), b2_sem.at[:, n, d], to_x[d]) for d in range(NX - 1)])
    late = {}

    def forward(n):
        arrived(step2[n])
        late[n] = same((groups[n], core), fwd_sem.at[:, n], sibling)

    def arrive(n):
        arrived([late[n]])

    def own_points():
        arrived(moved)

    return forward, arrive, own_points


def projection_sum(flights, place, others, to, part_ref, m_ref, out_ref, inbox, sems):
    core_in, ax_in, by_in, ay_in, bx_in, z_in = inbox
    core_sem, ax_sem, by_sem, ay_sem, bx_sem, z_sem, gz_sem, gy_sem, gc_sem = sems
    (row, core, x, y, z), (xs, ys, zs), (sibling, to_x, to_y, to_z) = place, others, to
    flying = []

    def send(src, dst, sem, peer):
        flying.append(flights.send(src, dst, sem, peer))

    def arrive():
        arrived(flying)
        flying.clear()

    def lanes_of(c_, y_):
        return pl.ds(pl.multiple_of(c_ * LHALF + y_ * BLK, BLK), BLK)

    def half(c_):
        return pl.ds(pl.multiple_of(c_ * LHALF, LHALF), LHALF)

    def eight(v):
        return pl.ds(pl.multiple_of(v * SUB, SUB), SUB)

    every, first, second = pl.ds(0, NX), pl.ds(0, TP), pl.ds(TP, TP)
    mine, tile = half(core), lanes_of(core, y)

    def over_cores():
        send(part_ref.at[:, :, half(1 - core)], core_in, core_sem, sibling)

    def over_x_and_y():
        arrive()
        m_ref[:, :, mine] = part_ref[:, :, mine] + core_in[...]
        for d in range(NX - 1):
            send(m_ref.at[xs[d], first, mine], ax_in.at[d], ax_sem.at[:, d], to_x[d])
        for d in range(NY - 1):
            send(m_ref.at[every, second, lanes_of(core, ys[d])], by_in.at[d], by_sem.at[:, d], to_y[d])

    def over_y_and_x():
        arrive()
        m_ref[x, first, mine] = m_ref[x, first, mine] + ax_in[0] + ax_in[1] + ax_in[2]
        m_ref[every, second, tile] = m_ref[every, second, tile] + by_in[0] + by_in[1] + by_in[2]
        for d in range(NY - 1):
            send(m_ref.at[x, first, lanes_of(core, ys[d])], ay_in.at[d], ay_sem.at[:, d], to_y[d])
        for d in range(NX - 1):
            send(m_ref.at[xs[d], second, tile], bx_in.at[d], bx_sem.at[:, d], to_x[d])

    def over_z():
        arrive()
        m_ref[x, first, tile] = m_ref[x, first, tile] + ay_in[0] + ay_in[1] + ay_in[2]
        m_ref[x, second, tile] = m_ref[x, second, tile] + bx_in[0] + bx_in[1] + bx_in[2]
        for d in range(NZ - 1):
            send(m_ref.at[x, eight(zs[d]), tile], z_in.at[d], z_sem.at[:, d], to_z[d])

    def back_over_z():
        arrive()
        total = m_ref[x, eight(z), tile]
        for d in range(NZ - 1):
            total = total + z_in[d]
        out_ref[eight(z), tile] = total * (1.0 / 256.0)
        for d in range(NZ - 1):
            send(out_ref.at[eight(z), tile], out_ref.at[eight(z), tile], gz_sem.at[:, d], to_z[d])

    def back_over_y():
        arrive()
        for d in range(NY - 1):
            send(out_ref.at[:, tile], out_ref.at[:, tile], gy_sem.at[:, d], to_y[d])

    def back_over_cores():
        arrive()
        send(out_ref.at[:, mine], out_ref.at[:, mine], gc_sem, sibling)

    return over_cores, over_x_and_y, over_y_and_x, over_z, back_over_z, back_over_y, back_over_cores, arrive


def factor_kernel(
    ids_ref, points_ref, targets_ref, fac_ref, proj_ref,
    xq_ref, own_ref, t_ref, pick_ref, hi_ref, lo_ref, low_ref, winv_ref, s_ref, col_ref, row_ref, diag_ref, kown_ref,
    part_ref, m_ref, moment_ref, *rest,
):
    where = neighbours()
    flights = Flights()
    forward, arrive, own_points = gather_pivots(
        flights, *where, ids_ref, points_ref, targets_ref, xq_ref, own_ref, t_ref, pick_ref, rest[:3], rest[3:14])
    summing = projection_sum(flights, *where, part_ref, m_ref, moment_ref, rest[14:20], rest[20:])

    def prepare(b):
        for r0, r1 in cuts(b * BLK, (b + 1) * BLK if b < NB else Q + OWN, BLK):
            v = xq_ref[b].reshape(BLK, E) if b < NB else own_ref[r0 - Q:r1 - Q, :]
            hi_ref[r0:r1, :], lo_ref[r0:r1, :] = split(v)
            norms = jnp.broadcast_to(jnp.sum(v * v, axis=1, keepdims=True), (BLK, BLK))
            col_ref[r0:r1, :] = norms
            if b < NB:
                row_ref[:, r0:r1] = jnp.transpose(norms)[0:SUB, :]

    def kern(r0, r1, c0, c1):
        cross = dot3(hi_ref[r0:r1, :], lo_ref[r0:r1, :], hi_ref[c0:c1, :], lo_ref[c0:c1, :])
        col = jnp.tile(col_ref[r0:r1, :], (1, (c1 - c0) // BLK))
        return jnp.exp((col + row_ref[0:1, c0:c1] - 2.0 * cross) * (-0.5 / E))

    def own_rows(c0, c1):
        kown_ref[:, c0:c1] = kern(Q, Q + OWN, c0, c1)

    def own_moment(c):
        part_ref[c] = lax.dot_general(
            t_ref[c], kown_ref[...], (((1,), (0,)), ((), ())), precision=HI, preferred_element_type=F32)

    def schur(r0, r1, k):
        c0, c1 = k * BLK, (k + 1) * BLK
        own = r0 >= Q
        v = kown_ref[:, c0:c1] if own else kern(r0, r1, c0, c1)
        if k > 0:
            v = v - dot_nt(fac_ref[:, 0:c0] if own else low_ref[r0:r1, 0:c0], low_ref[c0:c1, 0:c0])
        s_ref[k % 2, r0:r1, :] = v

    def panel(r0, r1, k):
        c0, c1 = k * BLK, (k + 1) * BLK
        v = dot_nt(s_ref[k % 2, r0:r1, :], winv_ref[k])
        if r0 < Q:
            low_ref[r0:r1, c0:c1] = v
        else:
            fac_ref[:, c0:c1] = v

    def project(k):
        c0, c1 = k * BLK, (k + 1) * BLK
        v = moment_ref[:, c0:c1]
        if k > 0:
            v = v - dot_nt(proj_ref[:, 0:c0], low_ref[c0:c1, 0:c0])
        proj_ref[:, c0:c1] = dot_nt(v, winv_ref[k])

    rows, columns = (lax.broadcasted_iota(jnp.int32, (BLK, BLK), d) for d in (0, 1))
    ridge = jnp.where(rows == columns, RIDGE, 0.0).astype(F32)

    def next_diagonal(k):
        r0, r1 = (k + 1) * BLK, (k + 2) * BLK
        v = kern(r0, r1, r0, r1) + ridge
        if k > 0:
            old = low_ref[r0:r1, 0:k * BLK]
            v = v - dot_nt(old, old)
        s_ref[k % 2, k * BLK:(k + 1) * BLK, :] = v

    def nothing():
        pass

    do = functools.partial
    def third_group_over():
        arrive(1)
        forward(2)

    def all_here():
        arrive(2)
        own_points()

    midway = {1: third_group_over, 3: summing[1], 4: summing[2], 5: summing[4], 6: summing[6]}
    at_end = {0: functools.partial(forward, 1), 1: all_here, 2: summing[0], 4: summing[3], 5: summing[5], 6: summing[7]}
    spans = [(b * BLK, (b + 1) * BLK) for b in range(NB)] + [(Q, Q + OWN)]
    columns_of = {span: 0 for span in spans}

    def advance(span, k):
        jobs = []
        while columns_of[span] <= k:
            c = columns_of[span]
            if c > 0:
                jobs.append(do(panel, *span, c - 1))
            jobs.append(do(schur, *span, c))
            columns_of[span] = c + 1
        return jobs

    forward(0)
    arrive(0)
    prepare(0)
    diag_ref[...] = kern(0, BLK, 0, BLK) + ridge
    for k in range(NB):
        c0, c1, c2 = k * BLK, (k + 1) * BLK, (k + 2) * BLK
        early, side = [], []
        if k == 0:
            early.append(do(prepare, 1))
        if k == 1:
            early.append(do(prepare, 2))
        if k == 2:
            early += [do(prepare, b) for b in range(4, NB + 1)]
            early += [do(own_rows, a, b) for a, b in cuts(0, Q, 256)]
            early += [do(own_moment, c) for c in range(NX)]
        if k + 1 < NB:
            side += advance(spans[k + 1], k) + [do(next_diagonal, k)]
        if k == 1:
            side = early + side + [do(prepare, 3)]
        if k > 1:
            for span in spans[min(k + 2, NB):] if k > 2 else spans[4:5]:
                side += advance(span, k)
        if k == NB - 1:
            side += [do(project, b) for b in range(NB - 1)]
        if k == 2:
            side = side[:2 * (k + 1)] + early + side[2 * (k + 1):]
            early = []
        elif k == 0:
            side, early = early + side, []

        def emit(row, value, k=k):
            winv_ref[k, row:row + 1, :] = value[0:1, :]

        chol_inverse([diag_ref[SUB * g:SUB * (g + 1), :] for g in range(BLK // SUB)], emit, side, midway.get(k, nothing), k == 1)
        if k + 1 < NB:
            panel(c1, c2, k)
            last = low_ref[c1:c2, c0:c1]
            diag_ref[...] = s_ref[k % 2, c0:c1, :] - dot_nt(last, last)
        at_end.get(k, nothing)()
    panel(Q, Q + OWN, NB - 1)
    project(NB - 1)
    for c in flights.started:
        c.wait_send()


def factor_call(pivots, points, targets):
    rows = Q + OWN
    dma = pltpu.SemaphoreType.DMA
    return pl.pallas_call(
        factor_kernel,
        out_shape=(jax.ShapeDtypeStruct((OWN, Q), F32), jax.ShapeDtypeStruct((TWIDE, Q), F32)),
        in_specs=[pl.BlockSpec(memory_space=VMEM)] * 3,
        out_specs=[pl.BlockSpec(memory_space=VMEM)] * 2,
        scratch_shapes=[
            VMEM((NZ, 2, NY, ROWS, E), F32), VMEM((OWN, E), F32), VMEM((NX, TWIDE, OWN), F32), VMEM((NZ, 2, NY, ROWS, WIDE), F32),
            VMEM((rows, E), BF16), VMEM((rows, E), BF16), VMEM((Q, Q), F32), VMEM((NB, BLK, BLK), F32), VMEM((2, rows, BLK), F32),
            VMEM((rows, BLK), F32), VMEM((SUB, Q), F32), VMEM((BLK, BLK), F32), VMEM((OWN, Q), F32),
            VMEM((NX, TWIDE, Q), F32), VMEM((NX, TWIDE, Q), F32), VMEM((TWIDE, Q), F32),
            VMEM((NZ, NY, ROWS, WIDE), F32), VMEM((NY - 1, NZ, ROWS, WIDE), F32), VMEM((NZ - 1, ROWS, WIDE), F32),
            dma((2, NX - 1)), dma((2, NX - 1)), dma((2,)), dma((2, NY - 1)), dma((2, NZ - 1)), dma((2, NZ - 1)),
            dma((2, 3, NX - 1)), dma((2, 3, NY - 1)), dma((2, 3, NY - 1)), dma((2, 3, NX - 1)), dma((2, 3)),
            VMEM((NX, TWIDE, LHALF), F32), VMEM((NX - 1, TP, LHALF), F32), VMEM((NY - 1, NX, TP, BLK), F32),
            VMEM((NY - 1, TP, BLK), F32), VMEM((NX - 1, TP, BLK), F32), VMEM((NZ - 1, SUB, BLK), F32),
            dma((2,)), dma((2, NX - 1)), dma((2, NY - 1)), dma((2, NY - 1)), dma((2, NX - 1)), dma((2, NZ - 1)), dma((2, NZ - 1)), dma((2, NY - 1)), dma((2,)),
        ],
        compiler_params=pltpu.CompilerParams(collective_id=0, has_side_effects=True, vmem_limit_bytes=48 << 20),
        name="factor",
    )(pivots, points, targets)


def shards(points, pivots, targets):
    factor, projection = factor_call(pivots, points, targets.T)
    return factor, projection.T


def solution(mesh):
    return jax.shard_map(
        shards,
        mesh=mesh,
        in_specs=(P("rows", "cols"), P(), P("rows", "cols")),
        out_specs=(P(("rows", "cols"), None), P(None, "cols")),
        check_vma=False,
    )
```

```python
import functools

import jax
import jax.numpy as jnp
from jax import lax
from jax.experimental import pallas as pl
from jax.experimental.pallas import tpu as pltpu
from jax.sharding import PartitionSpec as P

F32, BF16 = jnp.float32, jnp.bfloat16
MESH = pl.DeviceIdType.MESH
VMEM = pltpu.VMEM

HI = lax.Precision.HIGHEST
NT = (((1,), (1,)), ((), ()))
SUB, BLK, NB = 8, 128, 8
Q = NB * BLK
OWN = 256
RIDGE = 0.001
NZ, NY, NX = 8, 4, 4
E, TGT, LOCAL = 1024, 256, 1024
WIDE, TWIDE = E // NX, TGT // NX


def lanes(x, c):
    return jnp.broadcast_to(x[:, c:c + 1], (SUB, BLK))


def sublanes(x, s):
    return jnp.broadcast_to(x[s:s + 1, :], (SUB, BLK))


def small_factor(e):
    low, inv = {}, [None] * SUB
    for k in range(0, SUB, 2):
        a, b, c = e[k, k], e[k + 1, k], e[k + 1, k + 1]
        ra, rd = lax.rsqrt(a), lax.rsqrt(a * c - b * b)
        inv[k], inv[k + 1] = ra, a * ra * rd
        low[k + 1, k] = b * ra
        f = ra * rd
        for m in range(k + 2, SUB):
            low[m, k] = e[m, k] * ra
            low[m, k + 1] = (a * e[m, k + 1] - b * e[m, k]) * f
        for n in range(k + 2, SUB):
            for m in range(n, SUB):
                e[m, n] = e[m, n] - low[m, k] * low[n, k] - low[m, k + 1] * low[n, k + 1]
    return low, inv


def chol_inverse(a, emit, side, midway, late):
    groups = BLK // SUB
    lane = lax.broadcasted_iota(jnp.int32, (SUB, BLK), 1)
    sub = lax.broadcasted_iota(jnp.int32, (SUB, BLK), 0)
    w = [jnp.where(lane == sub + SUB * g, 1.0, 0.0).astype(F32) for g in range(groups)]
    side = list(side)
    for g in range(groups):
        cols = [lanes(a[g], SUB * g + k) for k in range(SUB)]
        low, inv = small_factor({(m, k): sublanes(cols[k], m) for k in range(SUB) for m in range(k, SUB)})
        us, ws = [], []
        for k in range(SUB):
            u, x = sublanes(a[g], k), sublanes(w[g], k)
            for j in range(k):
                u, x = u - us[j] * low[k, j], x - ws[j] * low[k, j]
            us.append(u * inv[k])
            ws.append(x * inv[k])
            emit(SUB * g + k, ws[k])
        for i in range(g + 1, groups):
            vs = []
            for k in range(SUB):
                v = lanes(a[i], SUB * g + k)
                for j in range(k):
                    v = v - vs[j] * low[k, j]
                vs.append(v * inv[k])
            ai, wi = a[i], w[i]
            for k in range(SUB):
                ai, wi = ai - vs[k] * us[k], wi - vs[k] * ws[k]
            a[i], w[i] = ai, wi
        take = 0 if late and g < groups // 2 else -(-len(side) // (groups - g))
        for job in side[:take]:
            job()
        side = side[take:]
        if g == groups // 2 - 1:
            midway()


def dot_nt(a, b, precision=HI):
    return lax.dot_general(a, b, NT, precision=precision, preferred_element_type=F32)


def split(x):
    hi = x.astype(BF16)
    return hi, (x - hi.astype(F32)).astype(BF16)


def dot3(ah, al, bh, bl):
    d = functools.partial(lax.dot_general, dimension_numbers=NT, preferred_element_type=F32)
    return d(ah, bh) + (d(ah, bl) + d(al, bh))


def cuts(lo, hi, step):
    return [(s, min(s + step, hi)) for s in range(lo, hi, step)]


TP = TWIDE // 2
ROWS = Q // (2 * NY * NZ)
LHALF = Q // 2


def neighbours():
    row, x = lax.axis_index("rows"), lax.axis_index("cols")
    core, y, z = row % 2, (row // 2) % NY, row // (2 * NY)

    def at(z_, y_, core_, x_):
        return ((z_ * NY + y_) * 2 + core_, x_)

    xs = [(x + d) % NX for d in range(1, NX)]
    ys = [(y + d) % NY for d in range(1, NY)]
    zs = [(z + d) % NZ for d in range(1, NZ)]
    sibling = at(z, y, 1 - core, x)
    to_x = [at(z, y, core, v) for v in xs]
    to_y = [at(z, v, core, x) for v in ys]
    to_z = [at(v, y, core, x) for v in zs]
    barrier = pltpu.get_barrier_semaphore()
    peers = [sibling] + to_x + to_y + to_z
    for peer in peers:
        pl.semaphore_signal(barrier, inc=1, device_id=peer, device_id_type=MESH)
    pl.semaphore_wait(barrier, len(peers))
    return (row, core, x, y, z), (xs, ys, zs), (sibling, to_x, to_y, to_z)


class Flights:
    def __init__(self):
        self.started = []

    def send(self, src, dst, sem, peer):
        c = pltpu.make_async_remote_copy(src_ref=src, dst_ref=dst, send_sem=sem.at[0], recv_sem=sem.at[1], device_id=peer, device_id_type=MESH)
        c.start()
        self.started.append(c)
        return c


def arrived(copies):
    for c in copies:
        c.wait_recv()


def picked_rows(ids_ref, points_ref, base, out_ref):
    x = points_ref[...]
    hi = x.astype(BF16)
    rest = x - hi.astype(F32)
    mid = rest.astype(BF16)
    low = (rest - mid.astype(F32)).astype(BF16)
    per_row = ids_ref.shape[1] // BLK
    spot = lax.broadcasted_iota(jnp.int32, (BLK, LOCAL), 1).astype(F32) + base.astype(F32)
    for b in range(NB):
        ids = ids_ref[b // per_row:b // per_row + 1, (b % per_row) * BLK:(b % per_row + 1) * BLK]
        column = jnp.transpose(jnp.broadcast_to(ids.astype(F32), (BLK, BLK)))
        hot = jnp.where(jnp.tile(column, (1, LOCAL // BLK)) == spot, 1.0, 0.0).astype(BF16)
        d = functools.partial(jnp.dot, preferred_element_type=F32)
        out_ref[b] = ((d(hot, hi) + d(hot, mid)) + d(hot, low)).reshape(2, NY, ROWS, WIDE)


def gather_pivots(flights, place, others, to, ids_ref, points_ref, targets_ref, xq_ref, own_ref, t_ref, pick, inbox, sems):
    (row, core, x, y, z), (xs, ys, zs), (sibling, to_x, to_y, to_z) = place, others, to
    from_core, from_y, from_z = inbox
    own_sem, tgt_sem, core_sem, y_sem, z_sem, gz_sem, a1_sem, b1_sem, a2_sem, b2_sem, fwd_sem = sems
    send = flights.send
    cols = pl.ds(pl.multiple_of(x * WIDE, WIDE), WIDE)

    def quarter(v):
        return pl.ds(pl.multiple_of(v * OWN, OWN), OWN)

    moved = []
    for d, v in enumerate(xs):
        moved.append(send(points_ref.at[quarter(v), :], own_ref.at[:, cols], own_sem.at[:, d], to_x[d]))
        moved.append(send(targets_ref.at[:, quarter(v)], t_ref.at[x], tgt_sem.at[:, d], to_x[d]))
    own_ref[:, cols] = points_ref[quarter(x), :]
    t_ref[x] = targets_ref[:, quarter(x)]
    picked_rows(ids_ref, points_ref, row * LOCAL, pick)

    arrived([send(pick.at[:, 1 - core], from_core, core_sem, sibling)])
    pick[:, core] = pick[:, core] + from_core[...]
    arrived([send(pick.at[:, core, ys[d]], from_y.at[d], y_sem.at[:, d], to_y[d]) for d in range(NY - 1)])
    pick[:, core, y] = pick[:, core, y] + from_y[0] + from_y[1] + from_y[2]
    arrived([send(pick.at[zs[d], core, y], from_z.at[d], z_sem.at[:, d], to_z[d]) for d in range(NZ - 1)])
    total = pick[z, core, y]
    for d in range(NZ - 1):
        total = total + from_z[d]
    xq_ref[z, core, y, :, cols] = total

    def same(place_, sem, peer):
        return send(xq_ref.at[place_], xq_ref.at[place_], sem, peer)

    arrived([same((z, core, y, slice(None), cols), gz_sem.at[:, d], to_z[d]) for d in range(NZ - 1)])
    first, second = pl.ds(0, SUB), pl.ds(SUB, SUB)
    groups = (pl.ds(0, 2), pl.ds(2, 2), pl.ds(4, NB - 4))
    step1, step2 = [], []
    for n, blocks in enumerate(groups):
        step1.append([same((blocks, core, y, first, cols), a1_sem.at[:, n, d], to_x[d]) for d in range(NX - 1)]
                     + [same((blocks, core, y, second, cols), b1_sem.at[:, n, d], to_y[d]) for d in range(NY - 1)])
    for n, blocks in enumerate(groups):
        arrived(step1[n])
        step2.append([same((blocks, core, y, first), a2_sem.at[:, n, d], to_y[d]) for d in range(NY - 1)]
                     + [same((blocks, core, slice(None), second, cols), b2_sem.at[:, n, d], to_x[d]) for d in range(NX - 1)])
    late = {}

    def forward(n):
        arrived(step2[n])
        late[n] = same((groups[n], core), fwd_sem.at[:, n], sibling)

    def arrive(n):
        arrived([late[n]])

    def own_points():
        arrived(moved)

    return forward, arrive, own_points


def projection_sum(flights, place, others, to, part_ref, m_ref, out_ref, inbox, sems):
    core_in, ax_in, by_in, ay_in, bx_in, z_in = inbox
    core_sem, ax_sem, by_sem, ay_sem, bx_sem, z_sem, gz_sem, gy_sem, gc_sem = sems
    (row, core, x, y, z), (xs, ys, zs), (sibling, to_x, to_y, to_z) = place, others, to
    flying = []

    def send(src, dst, sem, peer):
        flying.append(flights.send(src, dst, sem, peer))

    def arrive():
        arrived(flying)
        flying.clear()

    def lanes_of(c_, y_):
        return pl.ds(pl.multiple_of(c_ * LHALF + y_ * BLK, BLK), BLK)

    def half(c_):
        return pl.ds(pl.multiple_of(c_ * LHALF, LHALF), LHALF)

    def eight(v):
        return pl.ds(pl.multiple_of(v * SUB, SUB), SUB)

    every, first, second = pl.ds(0, NX), pl.ds(0, TP), pl.ds(TP, TP)
    mine, tile = half(core), lanes_of(core, y)

    def over_cores():
        send(part_ref.at[:, :, half(1 - core)], core_in, core_sem, sibling)

    def over_x_and_y():
        arrive()
        m_ref[:, :, mine] = part_ref[:, :, mine] + core_in[...]
        for d in range(NX - 1):
            send(m_ref.at[xs[d], first, mine], ax_in.at[d], ax_sem.at[:, d], to_x[d])
        for d in range(NY - 1):
            send(m_ref.at[every, second, lanes_of(core, ys[d])], by_in.at[d], by_sem.at[:, d], to_y[d])

    def over_y_and_x():
        arrive()
        m_ref[x, first, mine] = m_ref[x, first, mine] + ax_in[0] + ax_in[1] + ax_in[2]
        m_ref[every, second, tile] = m_ref[every, second, tile] + by_in[0] + by_in[1] + by_in[2]
        for d in range(NY - 1):
            send(m_ref.at[x, first, lanes_of(core, ys[d])], ay_in.at[d], ay_sem.at[:, d], to_y[d])
        for d in range(NX - 1):
            send(m_ref.at[xs[d], second, tile], bx_in.at[d], bx_sem.at[:, d], to_x[d])

    def over_z():
        arrive()
        m_ref[x, first, tile] = m_ref[x, first, tile] + ay_in[0] + ay_in[1] + ay_in[2]
        m_ref[x, second, tile] = m_ref[x, second, tile] + bx_in[0] + bx_in[1] + bx_in[2]
        for d in range(NZ - 1):
            send(m_ref.at[x, eight(zs[d]), tile], z_in.at[d], z_sem.at[:, d], to_z[d])

    def back_over_z():
        arrive()
        total = m_ref[x, eight(z), tile]
        for d in range(NZ - 1):
            total = total + z_in[d]
        out_ref[eight(z), tile] = total * (1.0 / 256.0)
        for d in range(NZ - 1):
            send(out_ref.at[eight(z), tile], out_ref.at[eight(z), tile], gz_sem.at[:, d], to_z[d])

    def back_over_y():
        arrive()
        for d in range(NY - 1):
            send(out_ref.at[:, tile], out_ref.at[:, tile], gy_sem.at[:, d], to_y[d])

    def back_over_cores():
        arrive()
        send(out_ref.at[:, mine], out_ref.at[:, mine], gc_sem, sibling)

    return over_cores, over_x_and_y, over_y_and_x, over_z, back_over_z, back_over_y, back_over_cores, arrive


def factor_kernel(
    ids_ref, points_ref, targets_ref, fac_ref, proj_ref,
    xq_ref, own_ref, t_ref, pick_ref, hi_ref, lo_ref, low_ref, winv_ref, s_ref, col_ref, row_ref, diag_ref, kown_ref,
    part_ref, m_ref, moment_ref, *rest,
):
    where = neighbours()
    flights = Flights()
    forward, arrive, own_points = gather_pivots(
        flights, *where, ids_ref, points_ref, targets_ref, xq_ref, own_ref, t_ref, pick_ref, rest[:3], rest[3:14])
    summing = projection_sum(flights, *where, part_ref, m_ref, moment_ref, rest[14:20], rest[20:])

    def prepare(b):
        for r0, r1 in cuts(b * BLK, (b + 1) * BLK if b < NB else Q + OWN, BLK):
            v = xq_ref[b].reshape(BLK, E) if b < NB else own_ref[r0 - Q:r1 - Q, :]
            hi_ref[r0:r1, :], lo_ref[r0:r1, :] = split(v)
            norms = jnp.broadcast_to(jnp.sum(v * v, axis=1, keepdims=True), (BLK, BLK))
            col_ref[r0:r1, :] = norms
            if b < NB:
                row_ref[:, r0:r1] = jnp.transpose(norms)[0:SUB, :]

    def kern(r0, r1, c0, c1):
        cross = dot3(hi_ref[r0:r1, :], lo_ref[r0:r1, :], hi_ref[c0:c1, :], lo_ref[c0:c1, :])
        col = jnp.tile(col_ref[r0:r1, :], (1, (c1 - c0) // BLK))
        return jnp.exp((col + row_ref[0:1, c0:c1] - 2.0 * cross) * (-0.5 / E))

    def own_rows(c0, c1):
        kown_ref[:, c0:c1] = kern(Q, Q + OWN, c0, c1)

    def own_moment(c):
        part_ref[c] = lax.dot_general(
            t_ref[c], kown_ref[...], (((1,), (0,)), ((), ())), precision=HI, preferred_element_type=F32)

    def schur(r0, r1, k):
        c0, c1 = k * BLK, (k + 1) * BLK
        own = r0 >= Q
        v = kown_ref[:, c0:c1] if own else kern(r0, r1, c0, c1)
        if k > 0:
            v = v - dot_nt(fac_ref[:, 0:c0] if own else low_ref[r0:r1, 0:c0], low_ref[c0:c1, 0:c0])
        s_ref[k % 2, r0:r1, :] = v

    def panel(r0, r1, k):
        c0, c1 = k * BLK, (k + 1) * BLK
        v = dot_nt(s_ref[k % 2, r0:r1, :], winv_ref[k])
        if r0 < Q:
            low_ref[r0:r1, c0:c1] = v
        else:
            fac_ref[:, c0:c1] = v

    def project(k):
        c0, c1 = k * BLK, (k + 1) * BLK
        v = moment_ref[:, c0:c1]
        if k > 0:
            v = v - dot_nt(proj_ref[:, 0:c0], low_ref[c0:c1, 0:c0])
        proj_ref[:, c0:c1] = dot_nt(v, winv_ref[k])

    rows, columns = (lax.broadcasted_iota(jnp.int32, (BLK, BLK), d) for d in (0, 1))
    ridge = jnp.where(rows == columns, RIDGE, 0.0).astype(F32)

    def next_diagonal(k):
        r0, r1 = (k + 1) * BLK, (k + 2) * BLK
        v = kern(r0, r1, r0, r1) + ridge
        if k > 0:
            old = low_ref[r0:r1, 0:k * BLK]
            v = v - dot_nt(old, old)
        s_ref[k % 2, k * BLK:(k + 1) * BLK, :] = v

    def nothing():
        pass

    do = functools.partial
    def third_group_over():
        arrive(1)
        forward(2)

    def all_here():
        arrive(2)
        own_points()

    midway = {1: third_group_over, 3: summing[1], 4: summing[2], 5: summing[4], 6: summing[6]}
    at_end = {0: functools.partial(forward, 1), 1: all_here, 2: summing[0], 4: summing[3], 5: summing[5], 6: summing[7]}
    spans = [(b * BLK, (b + 1) * BLK) for b in range(NB)] + [(Q, Q + OWN)]
    columns_of = {span: 0 for span in spans}

    def advance(span, k):
        jobs = []
        while columns_of[span] <= k:
            c = columns_of[span]
            if c > 0:
                jobs.append(do(panel, *span, c - 1))
            jobs.append(do(schur, *span, c))
            columns_of[span] = c + 1
        return jobs

    forward(0)
    arrive(0)
    prepare(0)
    diag_ref[...] = kern(0, BLK, 0, BLK) + ridge
    for k in range(NB):
        c0, c1, c2 = k * BLK, (k + 1) * BLK, (k + 2) * BLK
        early, side = [], []
        if k == 0:
            early.append(do(prepare, 1))
        if k == 1:
            early.append(do(prepare, 2))
        if k == 2:
            early += [do(prepare, b) for b in range(4, NB + 1)]
            early += [do(own_rows, a, b) for a, b in cuts(0, Q, 256)]
            early += [do(own_moment, c) for c in range(NX)]
        if k + 1 < NB:
            side += advance(spans[k + 1], k) + [do(next_diagonal, k)]
        if k == 1:
            side = early + side + [do(prepare, 3)]
        if k > 1:
            below = spans[k + 2:NB] if k > 2 else spans[4:5]
            for pair in (below[i:i + 2] for i in range(0, len(below), 2)):
                both = (pair[0][0], pair[-1][1])
                columns_of[both] = columns_of[pair[0]]
                side += advance(both, k)
                for span in pair:
                    columns_of[span] = k + 1
            if k > 2:
                side += advance(spans[NB], k)
        if k == NB - 1:
            side += [do(project, b) for b in range(NB - 1)]
        if k == 2:
            side = side[:2 * (k + 1)] + early + side[2 * (k + 1):]
            early = []
        elif k == 0:
            side, early = early + side, []

        def emit(row, value, k=k):
            winv_ref[k, row:row + 1, :] = value[0:1, :]

        chol_inverse([diag_ref[SUB * g:SUB * (g + 1), :] for g in range(BLK // SUB)], emit, side, midway.get(k, nothing), k == 1)
        if k + 1 < NB:
            panel(c1, c2, k)
            last = low_ref[c1:c2, c0:c1]
            diag_ref[...] = s_ref[k % 2, c0:c1, :] - dot_nt(last, last)
        at_end.get(k, nothing)()
    panel(Q, Q + OWN, NB - 1)
    project(NB - 1)
    for c in flights.started:
        c.wait_send()


def factor_call(pivots, points, targets):
    rows = Q + OWN
    dma = pltpu.SemaphoreType.DMA
    return pl.pallas_call(
        factor_kernel,
        out_shape=(jax.ShapeDtypeStruct((OWN, Q), F32), jax.ShapeDtypeStruct((TWIDE, Q), F32)),
        in_specs=[pl.BlockSpec(memory_space=VMEM)] * 3,
        out_specs=[pl.BlockSpec(memory_space=VMEM)] * 2,
        scratch_shapes=[
            VMEM((NZ, 2, NY, ROWS, E), F32), VMEM((OWN, E), F32), VMEM((NX, TWIDE, OWN), F32), VMEM((NZ, 2, NY, ROWS, WIDE), F32),
            VMEM((rows, E), BF16), VMEM((rows, E), BF16), VMEM((Q, Q), F32), VMEM((NB, BLK, BLK), F32), VMEM((2, rows, BLK), F32),
            VMEM((rows, BLK), F32), VMEM((SUB, Q), F32), VMEM((BLK, BLK), F32), VMEM((OWN, Q), F32),
            VMEM((NX, TWIDE, Q), F32), VMEM((NX, TWIDE, Q), F32), VMEM((TWIDE, Q), F32),
            VMEM((NZ, NY, ROWS, WIDE), F32), VMEM((NY - 1, NZ, ROWS, WIDE), F32), VMEM((NZ - 1, ROWS, WIDE), F32),
            dma((2, NX - 1)), dma((2, NX - 1)), dma((2,)), dma((2, NY - 1)), dma((2, NZ - 1)), dma((2, NZ - 1)),
            dma((2, 3, NX - 1)), dma((2, 3, NY - 1)), dma((2, 3, NY - 1)), dma((2, 3, NX - 1)), dma((2, 3)),
            VMEM((NX, TWIDE, LHALF), F32), VMEM((NX - 1, TP, LHALF), F32), VMEM((NY - 1, NX, TP, BLK), F32),
            VMEM((NY - 1, TP, BLK), F32), VMEM((NX - 1, TP, BLK), F32), VMEM((NZ - 1, SUB, BLK), F32),
            dma((2,)), dma((2, NX - 1)), dma((2, NY - 1)), dma((2, NY - 1)), dma((2, NX - 1)), dma((2, NZ - 1)), dma((2, NZ - 1)), dma((2, NY - 1)), dma((2,)),
        ],
        compiler_params=pltpu.CompilerParams(collective_id=0, has_side_effects=True, vmem_limit_bytes=48 << 20),
        name="factor",
    )(pivots, points, targets)


def shards(points, pivots, targets):
    factor, projection = factor_call(pivots, points, targets.T)
    return factor, projection.T


def solution(mesh):
    return jax.shard_map(
        shards,
        mesh=mesh,
        in_specs=(P("rows", "cols"), P(), P("rows", "cols")),
        out_specs=(P(("rows", "cols"), None), P(None, "cols")),
        check_vma=False,
    )
```
